256 devices in a mesh: dp: 4 (over x), mem: 64 (over z, y, core).
Axes of the slice: x: 4, y: 4, z: 8, core: 2. Of those that a mesh axis runs over, the one named last changes fastest.
Arguments:
- queries: bfloat16 [32768, 2048], P(('dp', 'mem')), may hold values from -8 to 8
- keys_local: bfloat16 [32768, 2048], P(('dp', 'mem')), may hold values from -8 to 8
- values_local: bfloat16 [32768, 2048], P(('dp', 'mem')), may hold values from -6 to 6
- mem_keys: bfloat16 [256, 16, 128, 128], P('mem'), may hold values from -8 to 8
- mem_values: bfloat16 [256, 16, 128, 128], P('mem'), may hold values from -6 to 6
- prev_keys: bfloat16 [2048, 128, 128], P(('dp', 'mem')), may hold values from -6 to 6
- prev_values: bfloat16 [2048, 128, 128], P(('dp', 'mem')), may hold values from -6 to 6
- gate_logit: float32 [16], replicated, may hold values from -2 to 2
- cotangent: bfloat16 [32768, 2048], P(('dp', 'mem')), may hold values from -4 to 4
- block_home: int32 [16, 256], replicated, may hold values from 0 to 255, as said below
- query_blocks: int32 [256, 16, 4], P(('dp', 'mem')), may hold values from 0 to 255, as said below
- write_slots: int32 [2048], P(('dp', 'mem')), may hold values from 0 to 255, as said below
Outputs:
- mixed: bfloat16 [32768, 2048], P(('dp', 'mem'))
- new_keys: bfloat16 [256, 16, 128, 128], P('mem')
- new_values: bfloat16 [256, 16, 128, 128], P('mem')
- gate_grad: float32 [16], replicated
The draws below stay inside these ranges and needn't reach their ends.
Inputs may be any that keep to these rules, and one draw needn't show every extreme that they name: Each row block_home[h] is a permutation of the storage blocks; storage block p lies on index p // 4 of mem. `query_blocks`: of the requests of one device (its tiles, all heads), at most 2 name blocks whose storage lies on one index of mem. `write_slots`: no two units are written to the same storage block of the same head. Of the units held by the 4 devices at one index of mem, at most 1 go to storage on one index of mem.
All inputs are finite; a program needn't handle non-finite values.
Results may differ from the reference program's by a relative error of at most 0.0047.
Values may be sent and summed in bfloat16 or wider, within the bound.
A program may use at most 128 MiB of HBM per device.

```python
import math
import jax
import jax.numpy as jnp
from jax import lax

HEADS = 16
HD = 128
BT = 128
TOPB = 4
BLK_DEV = 4
WR_DEV = 8
TILE_DEV = 1
TOKENS = 32768
TILES = 256
BLOCKS = 256
UNITS = 2048
CAP = 2
N_DP = 4
N_MEM = 64


def shared_home(key):
    head_keys = jax.random.split(key, HEADS)
    return jax.vmap(lambda head_key: jax.random.permutation(head_key, BLOCKS))(head_keys).astype(jnp.int32)


def pick_owners(key, slot_count, per_owner, wanted, hot_owner):
    slot_owner = jnp.arange(slot_count, dtype=jnp.int32) // per_owner
    is_hot = jnp.any(slot_owner[:, None] == hot_owner[None, :], axis=1)
    first, second = jax.random.split(key)
    scores = jax.random.randint(first, (slot_count,), 0, 2 ** 19) * slot_count + jnp.arange(slot_count, dtype=jnp.int32) + jnp.where(is_hot, 2 ** 30, 0)
    chosen = lax.top_k(scores, wanted)[1]
    return jax.random.permutation(second, slot_owner[chosen])


def draw_block_home(key, part):
    return shared_home(key)


def draw_query_blocks(key, part):
    inverse = jnp.argsort(shared_home(key), axis=1).astype(jnp.int32)
    key = jax.random.fold_in(key, 1)
    device_count = N_DP * N_MEM
    requests = TILE_DEV * HEADS * TOPB
    hot_key, owner_key, local_key = jax.random.split(key, 3)
    group_hot = jax.vmap(lambda group_key: jax.random.permutation(group_key, N_MEM)[:2])(jax.random.split(hot_key, N_DP))
    device_hot = jnp.repeat(group_hot, N_MEM, axis=0)
    owner_dev = jax.vmap(lambda device_key, hot_owner: pick_owners(device_key, N_MEM * CAP, CAP, requests, hot_owner))(jax.random.split(owner_key, device_count), device_hot)
    local_block = jax.random.randint(local_key, (device_count, requests), 0, BLK_DEV)
    storage = (owner_dev * BLK_DEV + local_block).reshape(TILES, HEADS, TOPB)
    head_grid = jnp.broadcast_to(jnp.arange(HEADS, dtype=jnp.int32)[None, :, None], (TILES, HEADS, TOPB))
    return inverse[head_grid, storage]


def draw_write_slots(key, part):
    inverse = jnp.argsort(shared_home(key), axis=1).astype(jnp.int32)
    key = jax.random.fold_in(key, 2)
    offset_key, relabel_key, twist_key = jax.random.split(key, 3)
    offset = jax.random.randint(offset_key, (), 0, N_MEM)
    relabel = jax.random.permutation(relabel_key, N_MEM).astype(jnp.int32)
    twists = jax.random.randint(twist_key, (N_MEM,), 0, BLK_DEV)
    group_grid = jnp.arange(N_DP, dtype=jnp.int32)[:, None, None]
    column_grid = jnp.arange(N_MEM, dtype=jnp.int32)[None, :, None]
    unit_grid = jnp.arange(WR_DEV, dtype=jnp.int32)[None, None, :]
    owner_dev = relabel[(column_grid + group_grid * WR_DEV + unit_grid + offset) % N_MEM]
    local_block = (group_grid + twists[owner_dev]) % BLK_DEV
    storage = owner_dev * BLK_DEV + local_block
    head_grid = jnp.broadcast_to((column_grid * WR_DEV + unit_grid) % HEADS, storage.shape)
    return inverse[head_grid, storage].reshape(UNITS)


def draw_queries(key, part):
    key = jax.random.fold_in(key, 3)
    base_draw = jnp.clip(jax.random.normal(key, (TOKENS, HEADS, HD), jnp.float32), -6.0, 6.0)
    return base_draw.reshape(TOKENS, HEADS * HD).astype(jnp.bfloat16)


def draw_keys_local(key, part):
    key = jax.random.fold_in(key, 4)
    base_draw = jnp.clip(jax.random.normal(key, (TOKENS, HEADS, HD), jnp.float32), -6.0, 6.0)
    return base_draw.reshape(TOKENS, HEADS * HD).astype(jnp.bfloat16)


def draw_mem_keys(key, part):
    key = jax.random.fold_in(key, 5)
    base_draw = jnp.clip(jax.random.normal(key, (BLOCKS, HEADS, BT, HD), jnp.float32), -6.0, 6.0)
    return base_draw.astype(jnp.bfloat16)


def draw_cotangent(key, part):
    key = jax.random.fold_in(key, 6)
    first = jax.random.fold_in(key, 0)
    rising = 1.0 + 2.0 * jnp.arange(TOKENS, dtype=jnp.float32) / (TOKENS - 1)
    base_draw = jnp.clip(jax.random.normal(first, (TOKENS, HEADS * HD), jnp.float32), -6.0, 6.0)
    return (base_draw * rising[:, None] / math.sqrt(TOKENS)).astype(jnp.bfloat16)


def block_levels(rng, dims, cuts, low, largest):
    loudness, own = 1.0, jax.random.fold_in(rng, 6)
    for axis_at, parts in cuts:
        heights = jnp.exp(jax.random.uniform(jax.random.fold_in(own, axis_at), (parts,), jnp.float32, low / len(cuts), largest / len(cuts)))
        loudness = loudness * jnp.repeat(heights, dims[axis_at] // parts).reshape([-1 if axis == axis_at else 1 for axis in range(len(dims))])
    return loudness


def bell_draw(rng, shape, deviation, most, pieces=(), held_as=jnp.bfloat16):
    values = deviation * jax.random.normal(rng, shape, jnp.float32)
    if pieces:
        values = values * block_levels(rng, shape, pieces, -0.22, 0.18)
    return jnp.clip(values, -most, most).astype(held_as)


def setup_inputs(seed: int = 0) -> dict:
    splits = jax.random.split(jax.random.key(seed), 13)
    queries = draw_queries(jax.random.fold_in(splits[12], 71), 0)
    keys_local = draw_keys_local(jax.random.fold_in(splits[12], 71), 0)
    values_local = bell_draw(splits[2], (TOKENS, HEADS * HD), 1.0, 6.0, ((0, 256),))
    mem_keys = draw_mem_keys(jax.random.fold_in(splits[12], 71), 0)
    mem_values = bell_draw(splits[4], (BLOCKS, HEADS, BT, HD), 1.0, 6.0, ((0, 64),))
    prev_keys = bell_draw(splits[5], (UNITS, BT, HD), 1.0, 6.0, ((0, 256),))
    prev_values = bell_draw(splits[6], (UNITS, BT, HD), 1.0, 6.0, ((0, 256),))
    gate_logit = jnp.clip(jax.random.uniform(splits[7], (HEADS,), jnp.float32, -2.0, 2.0), -2.0, 2.0)
    cotangent = draw_cotangent(jax.random.fold_in(splits[12], 71), 0)
    block_home = draw_block_home(jax.random.fold_in(splits[12], 71), 0)
    query_blocks = draw_query_blocks(jax.random.fold_in(splits[12], 71), 0)
    write_slots = draw_write_slots(jax.random.fold_in(splits[12], 71), 0)
    return dict(queries=queries, keys_local=keys_local, values_local=values_local, mem_keys=mem_keys, mem_values=mem_values, prev_keys=prev_keys, prev_values=prev_values, gate_logit=gate_logit, cotangent=cotangent, block_home=block_home, query_blocks=query_blocks, write_slots=write_slots)


def attend(query_rows, key_rows, values, allowed):
    scaling = 1.0 / math.sqrt(HD)
    scores = jnp.einsum('hqd,hkd->hqk', query_rows.astype(jnp.float32), key_rows.astype(jnp.float32)) * scaling
    scores = jnp.where(allowed, scores, -1e+30)
    shifted = jnp.exp(scores - lax.optimization_barrier(jnp.max(scores, axis=-1, keepdims=True)))
    weights = (shifted / lax.optimization_barrier(jnp.sum(shifted, axis=-1, keepdims=True))).astype(jnp.bfloat16)
    return jnp.einsum('hqk,hkd->hqd', weights.astype(jnp.float32), values.astype(jnp.float32))

def to_tiles(array):
    return array.reshape(TILES, BT, HEADS, HD).transpose(0, 2, 1, 3)

def reference(queries, keys_local, values_local, mem_keys, mem_values, prev_keys, prev_values, gate_logit, cotangent, block_home, query_blocks, write_slots):
    head_column = jnp.arange(HEADS, dtype=jnp.int32)[:, None]
    causal = jnp.arange(BT)[:, None] >= jnp.arange(BT)[None, :]

    def one_tile(inputs):
        query_rows, key_rows, value_rows, wanted = inputs
        storage = block_home[head_column, wanted]
        far_keys = mem_keys[storage, head_column].reshape(HEADS, TOPB * BT, HD)
        far_values = mem_values[storage, head_column].reshape(HEADS, TOPB * BT, HD)
        near_att = attend(query_rows, key_rows, value_rows, causal[None])
        recalled = attend(query_rows, far_keys, far_values, True)
        return (near_att, recalled)
    near_att, recalled = lax.map(one_tile, (to_tiles(queries), to_tiles(keys_local), to_tiles(values_local), query_blocks))
    sigmoid_gate = jax.nn.sigmoid(gate_logit)
    opening = sigmoid_gate[None, :, None, None]
    blended = opening * recalled + (1.0 - opening) * near_att
    mixed = blended.transpose(0, 2, 1, 3).reshape(TOKENS, HEADS * HD).astype(jnp.bfloat16)
    upstream = to_tiles(cotangent).astype(jnp.float32)
    gate_grad = sigmoid_gate * (1.0 - sigmoid_gate) * lax.optimization_barrier(jnp.sum(upstream * (recalled - near_att), axis=(0, 2, 3)))
    unit_index = jnp.arange(UNITS, dtype=jnp.int32)
    unit_head = unit_index % (N_MEM * WR_DEV) % HEADS
    target = block_home[unit_head, write_slots]
    new_keys = mem_keys.at[target, unit_head].set(prev_keys)
    new_values = mem_values.at[target, unit_head].set(prev_values)
    return (mixed, new_keys, new_values, gate_grad)
```

```python
import functools
import math

import jax
import jax.numpy as jnp
from jax import lax
from jax.experimental import pallas as pl
from jax.experimental.pallas import tpu as pltpu
from jax.sharding import PartitionSpec as P

MESH = pl.DeviceIdType.MESH
BF16, F32 = jnp.bfloat16, jnp.float32
NZ, NL, ND = 8, 8, 4
OFFSETS = (3, -4, 2, -3, 1, -2, -1, 0)
NONE = -1e30


def wrap(value, size):
    return lax.rem(value + 4 * size, size)


def codes(block_home, query_blocks, write_slots):
    group, place = lax.axis_index("dp"), lax.axis_index("mem")
    layer, lane = place // NL, place % NL
    row = lane // 2
    lanes = jnp.arange(256, dtype=jnp.int32)
    wanted = query_blocks.reshape(16, 4)
    storage = jnp.sum(
        jnp.where(wanted[:, :, None] == lanes, block_home[:, None, :], 0), axis=-1
    ).reshape(64)
    owner = storage // 4
    count = jnp.arange(64, dtype=jnp.int32)
    rank = jnp.sum(
        ((owner[:, None] == owner[None, :]) & (count[:, None] > count[None, :])).astype(jnp.int32),
        axis=1,
    )
    homes = lax.dynamic_slice_in_dim(block_home, (place % 2) * 8, 8, 0)
    written = jnp.sum(jnp.where(write_slots[:, None] == lanes, homes, 0), axis=-1)
    packed = jnp.concatenate([storage * 2 + rank, written])
    everyone = lax.all_gather(packed, ("dp", "mem"), axis=0, tiled=False).reshape(ND, 64, 72)

    asked = lax.dynamic_index_in_dim(everyone, group, 0, keepdims=False)[:, :64]
    request = count[None, :, None]
    slot = jnp.arange(2, dtype=jnp.int32)
    select = jnp.sum(
        jnp.where(
            (asked[:, :, None] // 8 == place) & (asked[:, :, None] % 2 == slot),
            (asked[:, :, None] // 2 % 4) * 16 + request // 4,
            0,
        ),
        axis=1,
    ).reshape(128)
    column = lax.dynamic_index_in_dim(asked.reshape(NZ, NL, 64), lane, 1, keepdims=False)
    found = jnp.where(column // 64 == layer, (column // 8) % 8 * 2 + column % 2, -1)
    sixteen = jnp.arange(16, dtype=jnp.int32)
    heads = jnp.sum(
        jnp.where(found[:, :, None] == sixteen, request // 4, 0), axis=1
    ).reshape(128)

    targets = everyone[:, :, 64:]
    units = lax.dynamic_index_in_dim(targets, place, 1, keepdims=False).reshape(32)
    to_row = (row + group + layer) % 4
    to = sixteen // 2 * NL + to_row * 2 + sixteen % 2
    send = jnp.sum(
        jnp.where(units[None, :] // 4 == to[:, None], jnp.arange(32, dtype=jnp.int32), 0), axis=1
    )
    source = jnp.arange(64, dtype=jnp.int32)
    via = (row - source % NL // 2 - source // NL + 16) % 4
    landing = (via * NL + source % NL) * 2 + source // NL // 4
    unit_head = (source[:, None] * 8 + jnp.arange(8, dtype=jnp.int32)) % 16
    slab = jnp.where(targets // 4 == place, targets % 4 * 16 + unit_head, -1)
    come = jnp.max(slab, axis=(0, 2))
    fetch = jnp.max(
        jnp.where(come[None, :] == source[:, None], landing[None, :], -1), axis=1
    )
    return select, heads, found.reshape(512), send, fetch


def kernel(
    select,
    heads,
    found,
    send,
    fetch,
    gate,
    q_ref,
    kl_ref,
    vl_ref,
    cot_ref,
    mk_ref,
    mv_ref,
    pk_ref,
    pv_ref,
    mixed_ref,
    nk_ref,
    nv_ref,
    part_ref,
    kv_out,
    kv_in,
    q_all,
    slot_o,
    slot_s,
    near_o,
    res_o,
    res_s,
    got_o,
    got_s,
    unit_all,
    w_out,
    w_mid,
    w_in,
    bar_unused,
    kv_send,
    kv_recv,
    q_send,
    q_recv,
    ro_send,
    ro_recv,
    rs_send,
    rs_recv,
    x_send,
    x_recv,
    wz_send,
    wz_recv,
    wy_send,
    wy_recv,
    wx_send,
    wx_recv,
):
    group, place = lax.axis_index("dp"), lax.axis_index("mem")
    layer, lane = lax.div(place, NL), lax.rem(place, NL)
    row = lax.div(lane, 2)
    scale = 1.0 / math.sqrt(128.0)

    def at(g, z, l):
        return (g, z * NL + l)

    def remote(src, dst, s, r, to):
        return pltpu.make_async_remote_copy(
            src_ref=src, dst_ref=dst, send_sem=s, recv_sem=r, device_id=to, device_id_type=MESH
        )

    barrier = pltpu.get_barrier_semaphore()

    @pl.loop(1, 8)
    def _(r):
        pl.semaphore_signal(barrier, inc=1, device_id=at(group, layer, wrap(lane + r, NL)), device_id_type=MESH)
        pl.semaphore_signal(barrier, inc=1, device_id=at(group, wrap(layer + r, NZ), lane), device_id_type=MESH)

    @pl.loop(1, 4)
    def _(r):
        pl.semaphore_signal(barrier, inc=1, device_id=at(wrap(group + r, ND), layer, lane), device_id_type=MESH)

    for h in range(16):
        q_all[layer, h] = q_ref[:, h * 128 : (h + 1) * 128]
    for u in range(8):
        unit_all[group, u, 0] = pk_ref[u]
        unit_all[group, u, 1] = pv_ref[u]
    pl.semaphore_wait(barrier, 17)

    def q_copy(hop, up):
        source = wrap(layer - hop if up else layer + hop, NZ)
        to = at(group, wrap(layer + (1 if up else -1), NZ), lane)
        k = 0 if up else 1
        return remote(
            q_all.at[source], q_all.at[source], q_send.at[k, hop], q_recv.at[k, hop], to
        )

    q_copy(0, True).start()
    q_copy(0, False).start()

    def x_copy(r):
        return remote(
            unit_all.at[group],
            unit_all.at[group],
            x_send.at[r],
            x_recv.at[r],
            at(wrap(group + r, ND), layer, lane),
        )

    @pl.loop(1, 4)
    def _(r):
        x_copy(r).start()

    def kv_copy(i, r):
        return remote(
            kv_out.at[i, r],
            kv_in.at[i, lane],
            kv_send.at[i, r],
            kv_recv.at[i, r],
            at(group, layer, wrap(lane + r, NL)),
        )

    for i, off in enumerate(OFFSETS):
        tile = wrap(layer + off, NZ)
        for k in range(2):
            code = select[(tile * NL + lane) * 2 + k]
            kv_in[i, lane, 0, k] = mk_ref[code]
            kv_in[i, lane, 1, k] = mv_ref[code]

        @pl.loop(1, 8)
        def _(r):
            for k in range(2):
                code = select[(tile * NL + wrap(lane + r, NL)) * 2 + k]
                kv_out[i, r, 0, k] = mk_ref[code]
                kv_out[i, r, 1, k] = mv_ref[code]
            kv_copy(i, r).start()

    def attend(qh, kh, vh, allowed=None):
        scores = (
            lax.dot_general(qh, kh, (((1,), (1,)), ((), ())), preferred_element_type=F32) * scale
        )
        if allowed is not None:
            scores = jnp.where(allowed, scores, NONE)
        top = jnp.max(scores, axis=1, keepdims=True)
        shifted = jnp.exp(scores - top)
        total = jnp.sum(shifted, axis=1, keepdims=True)
        out = jnp.dot(shifted.astype(BF16), vh, preferred_element_type=F32) / total
        return out, top + jnp.log(total)

    rows_at = lax.broadcasted_iota(jnp.int32, (128, 128), 0)
    cols_at = lax.broadcasted_iota(jnp.int32, (128, 128), 1)

    def near(first):
        @pl.loop(first, first + 8)
        def _(h):
            cols = pl.ds(pl.multiple_of(h * 128, 128), 128)
            out, _ = attend(q_ref[:, cols], kl_ref[:, cols], vl_ref[:, cols], rows_at >= cols_at)
            near_o[h] = out

    near(0)
    for hop in range(4):
        q_copy(hop, True).wait_recv()
        if hop < 3:
            q_copy(hop + 1, True).start()
            q_copy(hop, False).wait_recv()
        if hop < 2:
            q_copy(hop + 1, False).start()
        if hop == 0:
            near(8)
        if hop == 1:
            @pl.loop(1, 4)
            def _(r):
                x_copy(r).wait_recv()

            for r in range(8):
                to_layer = wrap(layer + r, NZ)
                for k in range(2):
                    unit = send[to_layer * 2 + k]
                    for kv in range(2):
                        slab = unit_all[unit // 8, unit % 8, kv]
                        if r == 0:
                            w_mid[k, lax.rem(layer, 4), lax.div(layer, 4), kv] = slab
                        else:
                            w_out[r, k, kv] = slab
                    if r > 0:
                        wz_copy_args = (
                            w_out.at[r, k],
                            w_mid.at[k, lax.rem(layer, 4), lax.div(layer, 4)],
                            wz_send.at[r, k],
                            wz_recv.at[r, k],
                            at(group, to_layer, lane),
                        )
                        remote(*wz_copy_args).start()

    def wz_copy(r, k):
        return remote(
            w_out.at[r, k],
            w_mid.at[k, lax.rem(layer, 4), lax.div(layer, 4)],
            wz_send.at[r, k],
            wz_recv.at[r, k],
            at(group, wrap(layer + r, NZ), lane),
        )

    def wy_copy(r):
        peer = wrap(lane + r, NL)
        low = wrap(lax.div(peer, 2) - row - group, 4)
        return remote(
            w_mid.at[lax.rem(peer, 2), low],
            w_in.at[group, lane],
            wy_send.at[r],
            wy_recv.at[r],
            at(group, layer, peer),
        )

    def wx_copy(r):
        return remote(
            w_in.at[group],
            w_in.at[group],
            wx_send.at[r],
            wx_recv.at[r],
            at(wrap(group + r, ND), layer, lane),
        )

    def result_copies(i):
        to = at(group, wrap(layer + (1 if OFFSETS[i] > 0 else -1), NZ), lane)
        return (
            remote(res_o.at[i], got_o.at[i], ro_send.at[i], ro_recv.at[i], to),
            remote(res_s.at[i], got_s.at[i], rs_send.at[i], rs_recv.at[i], to),
        )

    joins = []
    for i, off in enumerate(OFFSETS):
        if off == 0:
            joins.append((OFFSETS.index(1), OFFSETS.index(-1)))
        else:
            further = off + (1 if off > 0 else -1)
            joins.append((OFFSETS.index(further),) if further in OFFSETS else ())

    for i, off in enumerate(OFFSETS):
        tile = wrap(layer + off, NZ)

        @pl.loop(1, 8)
        def _(r):
            kv_copy(i, r).wait_recv()

        @pl.loop(0, 4)
        def _(step):
            for k in range(4):
                s = step * 4 + k
                head = heads[tile * 16 + s]
                kh, vh = kv_in[i, step * 2 + k // 2, 0, k % 2], kv_in[i, step * 2 + k // 2, 1, k % 2]
                out, stat = attend(q_all[tile, head], kh, vh)
                slot_o[s] = out
                slot_s[s] = jnp.broadcast_to(stat, (128, 128))

        for j in joins[i]:
            for copy in result_copies(j):
                copy.wait_recv()
        if off != 0:
            res_s[i] = jnp.full((128, 128), NONE, F32)

        @pl.loop(0, 16)
        def _(h):
            outs, stats = [], []
            for j in range(4):
                where = found[tile * 64 + h * 4 + j]
                spot = jnp.maximum(where, 0)
                outs.append(slot_o[spot])
                stats.append(jnp.where(where >= 0, slot_s[spot], NONE))
            for j in joins[i]:
                outs.append(got_o[j, h].astype(F32))
                stat = jnp.sum(jnp.where(cols_at == h, got_s[j], 0.0), axis=1, keepdims=True)
                stats.append(jnp.broadcast_to(stat, (128, 128)))
            top = functools.reduce(jnp.maximum, stats)
            weights = [jnp.exp(stat - top) for stat in stats]
            total = functools.reduce(jnp.add, weights)
            out = functools.reduce(jnp.add, [w * o for w, o in zip(weights, outs)]) / total
            if off != 0:
                res_o[i, h] = out.astype(BF16)
                res_s[i] = jnp.where(cols_at == h, top + jnp.log(total), res_s[i])
            else:
                cols = pl.ds(pl.multiple_of(h * 128, 128), 128)
                opening = gate[h]
                local = near_o[h]
                mixed_ref[:, cols] = (opening * out + (1.0 - opening) * local).astype(BF16)
                part_ref[pl.ds(h, 1), :] = jnp.sum(
                    cot_ref[:, cols].astype(F32) * (out - local), axis=0, keepdims=True
                )

        if off != 0:
            for copy in result_copies(i):
                copy.start()
        if i == 1:
            @pl.loop(1, 8)
            def _(r):
                for k in range(2):
                    wz_copy(r, k).wait_recv()

            low = wrap(-group, 4)
            w_in[group, lane] = w_mid[lax.rem(lane, 2), low]

            @pl.loop(1, 8)
            def _(r):
                wy_copy(r).start()

        if i == 3:
            @pl.loop(1, 8)
            def _(r):
                wy_copy(r).wait_recv()

            @pl.loop(1, 4)
            def _(r):
                wx_copy(r).start()

    @pl.loop(1, 4)
    def _(r):
        wx_copy(r).wait_recv()

    @pl.loop(0, 64)
    def _(slab):
        where = fetch[slab]
        spot = jnp.maximum(where, 0)
        for kv, (old, new) in enumerate(((mk_ref, nk_ref), (mv_ref, nv_ref))):
            came = w_in[spot // 16, spot // 2 % 8, spot % 2, kv]
            new[slab] = jnp.where(where >= 0, came, old[slab])

    for hop in range(4):
        q_copy(hop, True).wait_send()
        if hop < 3:
            q_copy(hop, False).wait_send()
    for i, off in enumerate(OFFSETS):
        if off != 0:
            for copy in result_copies(i):
                copy.wait_send()

        @pl.loop(1, 8)
        def _(r):
            kv_copy(i, r).wait_send()

    @pl.loop(1, 4)
    def _(r):
        x_copy(r).wait_send()
        wx_copy(r).wait_send()

    @pl.loop(1, 8)
    def _(r):
        wy_copy(r).wait_send()
        for k in range(2):
            wz_copy(r, k).wait_send()


def on_device(
    queries,
    keys_local,
    values_local,
    mem_keys,
    mem_values,
    prev_keys,
    prev_values,
    gate_logit,
    cotangent,
    block_home,
    query_blocks,
    write_slots,
):
    tables = codes(block_home, query_blocks, write_slots)
    sigmoid_gate = jax.nn.sigmoid(gate_logit)
    smem, vmem = (pl.BlockSpec(memory_space=space) for space in (pltpu.SMEM, pltpu.VMEM))
    dma = pltpu.SemaphoreType.DMA
    mixed, new_keys, new_values, part = pl.pallas_call(
        kernel,
        out_shape=(
            jax.ShapeDtypeStruct((128, 2048), BF16),
            jax.ShapeDtypeStruct((64, 128, 128), BF16),
            jax.ShapeDtypeStruct((64, 128, 128), BF16),
            jax.ShapeDtypeStruct((16, 128), F32),
        ),
        in_specs=[smem] * 6 + [vmem] * 8,
        out_specs=(vmem,) * 4,
        scratch_shapes=[
            pltpu.VMEM((8, 8, 2, 2, 128, 128), BF16),
            pltpu.VMEM((8, 8, 2, 2, 128, 128), BF16),
            pltpu.VMEM((8, 16, 128, 128), BF16),
            pltpu.VMEM((16, 128, 128), F32),
            pltpu.VMEM((16, 128, 128), F32),
            pltpu.VMEM((16, 128, 128), F32),
            pltpu.VMEM((7, 16, 128, 128), BF16),
            pltpu.VMEM((7, 128, 128), F32),
            pltpu.VMEM((7, 16, 128, 128), BF16),
            pltpu.VMEM((7, 128, 128), F32),
            pltpu.VMEM((4, 8, 2, 128, 128), BF16),
            pltpu.VMEM((8, 2, 2, 128, 128), BF16),
            pltpu.VMEM((2, 4, 2, 2, 128, 128), BF16),
            pltpu.VMEM((4, 8, 2, 2, 128, 128), BF16),
            pltpu.SMEM((1,), jnp.int32),
            dma((8, 8)),
            dma((8, 8)),
            dma((2, 4)),
            dma((2, 4)),
            dma((7,)),
            dma((7,)),
            dma((7,)),
            dma((7,)),
            dma((4,)),
            dma((4,)),
            dma((8, 2)),
            dma((8, 2)),
            dma((8,)),
            dma((8,)),
            dma((4,)),
            dma((4,)),
        ],
        compiler_params=pltpu.CompilerParams(
            collective_id=0, has_side_effects=True, vmem_limit_bytes=60 * 1024 * 1024
        ),
    )(
        *tables,
        sigmoid_gate,
        queries,
        keys_local,
        values_local,
        cotangent,
        mem_keys.reshape(64, 128, 128),
        mem_values.reshape(64, 128, 128),
        prev_keys,
        prev_values,
    )
    total = lax.psum(jnp.sum(part, axis=1), ("dp", "mem"))
    gate_grad = sigmoid_gate * (1.0 - sigmoid_gate) * total
    return mixed, new_keys.reshape(mem_keys.shape), new_values.reshape(mem_values.shape), gate_grad


def solution(mesh):
    tokens, slabs = P(("dp", "mem"), None), P("mem", None, None, None)
    units = P(("dp", "mem"), None, None)
    return jax.shard_map(
        on_device,
        mesh=mesh,
        in_specs=(
            tokens,
            tokens,
            tokens,
            slabs,
            slabs,
            units,
            units,
            P(),
            tokens,
            P(),
            units,
            P(("dp", "mem")),
        ),
        out_specs=(tokens, slabs, slabs, P()),
        check_vma=False,
    )
```

```python
import functools
import math

import jax
import jax.numpy as jnp
from jax import lax
from jax.experimental import pallas as pl
from jax.experimental.pallas import tpu as pltpu
from jax.sharding import PartitionSpec as P

MESH = pl.DeviceIdType.MESH
BF16, F32 = jnp.bfloat16, jnp.float32
NZ, NL, ND = 8, 8, 4
OFFSETS = (3, -4, 2, -3, 1, -2, -1, 0)
NONE = -1e30


def wrap(value, size):
    return lax.rem(value + 4 * size, size)


def peers(group, layer, lane):
    in_layer = lambda r: (group, layer * NL + wrap(lane + r, NL))
    along_z = lambda r: (group, wrap(layer + r, NZ) * NL + lane)
    in_groups = lambda r: (wrap(group + r, ND), layer * NL + lane)
    return in_layer, along_z, in_groups


def greet(group, layer, lane):
    barrier = pltpu.get_barrier_semaphore()
    in_layer, along_z, in_groups = peers(group, layer, lane)

    @pl.loop(1, 8)
    def _(r):
        pl.semaphore_signal(barrier, inc=1, device_id=in_layer(r), device_id_type=MESH)
        pl.semaphore_signal(barrier, inc=1, device_id=along_z(r), device_id_type=MESH)

    @pl.loop(1, 4)
    def _(r):
        pl.semaphore_signal(barrier, inc=1, device_id=in_groups(r), device_id_type=MESH)

    return lambda: pl.semaphore_wait(barrier, 17)


def remote(src, dst, s, r, to):
    return pltpu.make_async_remote_copy(
        src_ref=src, dst_ref=dst, send_sem=s, recv_sem=r, device_id=to, device_id_type=MESH
    )


def code_kernel(own, out, x_send, x_recv, l_send, l_recv, z_send, z_recv):
    group, place = lax.axis_index("dp"), lax.axis_index("mem")
    layer, lane = lax.div(place, NL), lax.rem(place, NL)
    in_layer, along_z, in_groups = peers(group, layer, lane)
    ready = greet(group, layer, lane)
    out[layer, lane, group] = own[...]
    ready()
    for part, size, s, r, to in (
        (out.at[layer, lane, group], ND, x_send, x_recv, in_groups),
        (out.at[layer, lane], NL, l_send, l_recv, in_layer),
        (out.at[layer], NZ, z_send, z_recv, along_z),
    ):
        copies = [remote(part, part, s.at[k], r.at[k], to(k)) for k in range(1, size)]
        for copy in copies:
            copy.start()
        for copy in copies:
            copy.wait()


def gather_codes(own):
    dma = pltpu.SemaphoreType.DMA
    vmem = pl.BlockSpec(memory_space=pltpu.VMEM)
    return pl.pallas_call(
        code_kernel,
        out_shape=jax.ShapeDtypeStruct((NZ, NL, ND, 1, 128), jnp.int32),
        in_specs=[vmem],
        out_specs=vmem,
        scratch_shapes=[dma((ND,)), dma((ND,)), dma((NL,)), dma((NL,)), dma((NZ,)), dma((NZ,))],
        compiler_params=pltpu.CompilerParams(collective_id=1, has_side_effects=True),
    )(own)


def codes(block_home, query_blocks, write_slots):
    group, place = lax.axis_index("dp"), lax.axis_index("mem")
    layer, lane = place // NL, place % NL
    row = lane // 2
    lanes = jnp.arange(256, dtype=jnp.int32)
    wanted = query_blocks.reshape(16, 4)
    storage = jnp.sum(
        jnp.where(wanted[:, :, None] == lanes, block_home[:, None, :], 0), axis=-1
    ).reshape(64)
    owner = storage // 4
    count = jnp.arange(64, dtype=jnp.int32)
    rank = jnp.sum(
        ((owner[:, None] == owner[None, :]) & (count[:, None] > count[None, :])).astype(jnp.int32),
        axis=1,
    )
    homes = lax.dynamic_slice_in_dim(block_home, (place % 2) * 8, 8, 0)
    written = jnp.sum(jnp.where(write_slots[:, None] == lanes, homes, 0), axis=-1)
    packed = jnp.concatenate([storage * 2 + rank, written, jnp.zeros((56,), jnp.int32)])
    everyone = gather_codes(packed.reshape(1, 128)).reshape(64, ND, 128)[:, :, :72]
    everyone = everyone.transpose(1, 0, 2)

    asked = lax.dynamic_index_in_dim(everyone, group, 0, keepdims=False)[:, :64]
    request = count[None, :, None]
    slot = jnp.arange(2, dtype=jnp.int32)
    select = jnp.sum(
        jnp.where(
            (asked[:, :, None] // 8 == place) & (asked[:, :, None] % 2 == slot),
            (asked[:, :, None] // 2 % 4) * 16 + request // 4,
            0,
        ),
        axis=1,
    ).reshape(128)
    column = lax.dynamic_index_in_dim(asked.reshape(NZ, NL, 64), lane, 1, keepdims=False)
    found = jnp.where(column // 64 == layer, (column // 8) % 8 * 2 + column % 2, -1)
    sixteen = jnp.arange(16, dtype=jnp.int32)
    heads = jnp.sum(
        jnp.where(found[:, :, None] == sixteen, request // 4, 0), axis=1
    ).reshape(128)

    targets = everyone[:, :, 64:]
    units = lax.dynamic_index_in_dim(targets, place, 1, keepdims=False).reshape(32)
    to_row = (row + group + layer) % 4
    to = sixteen // 2 * NL + to_row * 2 + sixteen % 2
    send = jnp.sum(
        jnp.where(units[None, :] // 4 == to[:, None], jnp.arange(32, dtype=jnp.int32), 0), axis=1
    )
    source = jnp.arange(64, dtype=jnp.int32)
    via = (row - source % NL // 2 - source // NL + 16) % 4
    landing = (via * NL + source % NL) * 2 + source // NL // 4
    unit_head = (source[:, None] * 8 + jnp.arange(8, dtype=jnp.int32)) % 16
    slab = jnp.where(targets // 4 == place, targets % 4 * 16 + unit_head, -1)
    come = jnp.max(slab, axis=(0, 2))
    fetch = jnp.max(
        jnp.where(come[None, :] == source[:, None], landing[None, :], -1), axis=1
    )
    return select, heads, found.reshape(512), send, fetch


def kernel(
    select,
    heads,
    found,
    send,
    fetch,
    gate,
    q_ref,
    kl_ref,
    vl_ref,
    cot_ref,
    mk_ref,
    mv_ref,
    pk_ref,
    pv_ref,
    mixed_ref,
    nk_ref,
    nv_ref,
    part_ref,
    kv_out,
    kv_in,
    q_all,
    slot_o,
    slot_s,
    near_o,
    res_o,
    res_s,
    got_o,
    got_s,
    unit_all,
    w_out,
    w_mid,
    w_in,
    part,
    g_x,
    g_l,
    g_z,
    kv_send,
    kv_recv,
    q_send,
    q_recv,
    ro_send,
    ro_recv,
    rs_send,
    rs_recv,
    x_send,
    x_recv,
    wz_send,
    wz_recv,
    wy_send,
    wy_recv,
    wx_send,
    wx_recv,
    gx_send,
    gx_recv,
    gl_send,
    gl_recv,
    gz_send,
    gz_recv,
):
    group, place = lax.axis_index("dp"), lax.axis_index("mem")
    layer, lane = lax.div(place, NL), lax.rem(place, NL)
    row = lax.div(lane, 2)
    scale = 1.0 / math.sqrt(128.0)

    def at(g, z, l):
        return (g, z * NL + l)

    ready = greet(group, layer, lane)
    for h in range(16):
        q_all[layer, h] = q_ref[:, h * 128 : (h + 1) * 128]
    for u in range(8):
        unit_all[group, u, 0] = pk_ref[u]
        unit_all[group, u, 1] = pv_ref[u]
    ready()

    def q_copy(hop, up):
        source = wrap(layer - hop if up else layer + hop, NZ)
        to = at(group, wrap(layer + (1 if up else -1), NZ), lane)
        k = 0 if up else 1
        return remote(
            q_all.at[source], q_all.at[source], q_send.at[k, hop], q_recv.at[k, hop], to
        )

    q_copy(0, True).start()
    q_copy(0, False).start()

    def x_copy(r):
        return remote(
            unit_all.at[group],
            unit_all.at[group],
            x_send.at[r],
            x_recv.at[r],
            at(wrap(group + r, ND), layer, lane),
        )

    @pl.loop(1, 4)
    def _(r):
        x_copy(r).start()

    def kv_copy(i, r):
        return remote(
            kv_out.at[i, r],
            kv_in.at[i, lane],
            kv_send.at[i, r],
            kv_recv.at[i, r],
            at(group, layer, wrap(lane + r, NL)),
        )

    for i, off in enumerate(OFFSETS):
        tile = wrap(layer + off, NZ)
        for k in range(2):
            code = select[(tile * NL + lane) * 2 + k]
            kv_in[i, lane, 0, k] = mk_ref[code]
            kv_in[i, lane, 1, k] = mv_ref[code]

        @pl.loop(1, 8)
        def _(r):
            for k in range(2):
                code = select[(tile * NL + wrap(lane + r, NL)) * 2 + k]
                kv_out[i, r, 0, k] = mk_ref[code]
                kv_out[i, r, 1, k] = mv_ref[code]
            kv_copy(i, r).start()

    def attend(qh, kh, vh, allowed=None):
        scores = (
            lax.dot_general(qh, kh, (((1,), (1,)), ((), ())), preferred_element_type=F32) * scale
        )
        if allowed is not None:
            scores = jnp.where(allowed, scores, NONE)
        top = jnp.max(scores, axis=1, keepdims=True)
        shifted = jnp.exp(scores - top)
        total = jnp.sum(shifted, axis=1, keepdims=True)
        out = jnp.dot(shifted.astype(BF16), vh, preferred_element_type=F32) / total
        return out, top + jnp.log(total)

    rows_at = lax.broadcasted_iota(jnp.int32, (128, 128), 0)
    cols_at = lax.broadcasted_iota(jnp.int32, (128, 128), 1)

    def near(first):
        @pl.loop(first, first + 8)
        def _(h):
            cols = pl.ds(pl.multiple_of(h * 128, 128), 128)
            out, _ = attend(q_ref[:, cols], kl_ref[:, cols], vl_ref[:, cols], rows_at >= cols_at)
            near_o[h] = out

    near(0)
    for hop in range(4):
        q_copy(hop, True).wait_recv()
        if hop < 3:
            q_copy(hop + 1, True).start()
            q_copy(hop, False).wait_recv()
        if hop < 2:
            q_copy(hop + 1, False).start()
        if hop == 0:
            near(8)
        if hop == 1:
            @pl.loop(1, 4)
            def _(r):
                x_copy(r).wait_recv()

            for r in range(8):
                to_layer = wrap(layer + r, NZ)
                for k in range(2):
                    unit = send[to_layer * 2 + k]
                    for kv in range(2):
                        slab = unit_all[unit // 8, unit % 8, kv]
                        if r == 0:
                            w_mid[k, lax.rem(layer, 4), lax.div(layer, 4), kv] = slab
                        else:
                            w_out[r, k, kv] = slab
                    if r > 0:
                        wz_copy_args = (
                            w_out.at[r, k],
                            w_mid.at[k, lax.rem(layer, 4), lax.div(layer, 4)],
                            wz_send.at[r, k],
                            wz_recv.at[r, k],
                            at(group, to_layer, lane),
                        )
                        remote(*wz_copy_args).start()

    def wz_copy(r, k):
        return remote(
            w_out.at[r, k],
            w_mid.at[k, lax.rem(layer, 4), lax.div(layer, 4)],
            wz_send.at[r, k],
            wz_recv.at[r, k],
            at(group, wrap(layer + r, NZ), lane),
        )

    def wy_copy(r):
        peer = wrap(lane + r, NL)
        low = wrap(lax.div(peer, 2) - row - group, 4)
        return remote(
            w_mid.at[lax.rem(peer, 2), low],
            w_in.at[group, lane],
            wy_send.at[r],
            wy_recv.at[r],
            at(group, layer, peer),
        )

    def wx_copy(r):
        return remote(
            w_in.at[group],
            w_in.at[group],
            wx_send.at[r],
            wx_recv.at[r],
            at(wrap(group + r, ND), layer, lane),
        )

    def result_copies(i):
        to = at(group, wrap(layer + (1 if OFFSETS[i] > 0 else -1), NZ), lane)
        return (
            remote(res_o.at[i], got_o.at[i], ro_send.at[i], ro_recv.at[i], to),
            remote(res_s.at[i], got_s.at[i], rs_send.at[i], rs_recv.at[i], to),
        )

    joins = []
    for i, off in enumerate(OFFSETS):
        if off == 0:
            joins.append((OFFSETS.index(1), OFFSETS.index(-1)))
        else:
            further = off + (1 if off > 0 else -1)
            joins.append((OFFSETS.index(further),) if further in OFFSETS else ())

    for i, off in enumerate(OFFSETS):
        tile = wrap(layer + off, NZ)

        @pl.loop(1, 8)
        def _(r):
            kv_copy(i, r).wait_recv()

        @pl.loop(0, 4)
        def _(step):
            for k in range(4):
                s = step * 4 + k
                head = heads[tile * 16 + s]
                kh, vh = kv_in[i, step * 2 + k // 2, 0, k % 2], kv_in[i, step * 2 + k // 2, 1, k % 2]
                out, stat = attend(q_all[tile, head], kh, vh)
                slot_o[s] = out
                slot_s[s] = jnp.broadcast_to(stat, (128, 128))

        for j in joins[i]:
            for copy in result_copies(j):
                copy.wait_recv()
        if off != 0:
            res_s[i] = jnp.full((128, 128), NONE, F32)

        @pl.loop(0, 16)
        def _(h):
            outs, stats = [], []
            for j in range(4):
                where = found[tile * 64 + h * 4 + j]
                spot = jnp.maximum(where, 0)
                outs.append(slot_o[spot])
                stats.append(jnp.where(where >= 0, slot_s[spot], NONE))
            for j in joins[i]:
                outs.append(got_o[j, h].astype(F32))
                stat = jnp.sum(jnp.where(cols_at == h, got_s[j], 0.0), axis=1, keepdims=True)
                stats.append(jnp.broadcast_to(stat, (128, 128)))
            top = functools.reduce(jnp.maximum, stats)
            weights = [jnp.exp(stat - top) for stat in stats]
            total = functools.reduce(jnp.add, weights)
            out = functools.reduce(jnp.add, [w * o for w, o in zip(weights, outs)]) / total
            if off != 0:
                res_o[i, h] = out.astype(BF16)
                res_s[i] = jnp.where(cols_at == h, top + jnp.log(total), res_s[i])
            else:
                cols = pl.ds(pl.multiple_of(h * 128, 128), 128)
                opening = gate[h]
                local = near_o[h]
                mixed_ref[:, cols] = (opening * out + (1.0 - opening) * local).astype(BF16)
                part[pl.ds(h, 1), :] = jnp.sum(
                    cot_ref[:, cols].astype(F32) * (out - local), axis=0, keepdims=True
                )

        if off != 0:
            for copy in result_copies(i):
                copy.start()
        if i == 1:
            @pl.loop(1, 8)
            def _(r):
                for k in range(2):
                    wz_copy(r, k).wait_recv()

            low = wrap(-group, 4)
            w_in[group, lane] = w_mid[lax.rem(lane, 2), low]

            @pl.loop(1, 8)
            def _(r):
                wy_copy(r).start()

        if i == 3:
            @pl.loop(1, 8)
            def _(r):
                wy_copy(r).wait_recv()

            @pl.loop(1, 4)
            def _(r):
                wx_copy(r).start()

    in_layer, along_z, in_groups = peers(group, layer, lane)

    def spread(value, held, mine, size, s, r, to):
        held[mine] = value
        copies = [
            remote(held.at[mine], held.at[mine], s.at[k], r.at[k], to(k)) for k in range(1, size)
        ]
        for copy in copies:
            copy.start()
        return copies

    def total_of(held, copies):
        for copy in copies:
            copy.wait()
        return jnp.sum(held[...], axis=0)

    gx = spread(part[...], g_x, group, ND, gx_send, gx_recv, in_groups)

    @pl.loop(1, 4)
    def _(r):
        wx_copy(r).wait_recv()

    gl = spread(total_of(g_x, gx), g_l, lane, NL, gl_send, gl_recv, in_layer)

    @pl.loop(0, 64)
    def _(slab):
        where = fetch[slab]
        spot = jnp.maximum(where, 0)
        for kv, (old, new) in enumerate(((mk_ref, nk_ref), (mv_ref, nv_ref))):
            came = w_in[spot // 16, spot // 2 % 8, spot % 2, kv]
            new[slab] = jnp.where(where >= 0, came, old[slab])

    gz = spread(total_of(g_l, gl), g_z, layer, NZ, gz_send, gz_recv, along_z)

    for hop in range(4):
        q_copy(hop, True).wait_send()
        if hop < 3:
            q_copy(hop, False).wait_send()
    for i, off in enumerate(OFFSETS):
        if off != 0:
            for copy in result_copies(i):
                copy.wait_send()

        @pl.loop(1, 8)
        def _(r):
            kv_copy(i, r).wait_send()

    @pl.loop(1, 4)
    def _(r):
        x_copy(r).wait_send()
        wx_copy(r).wait_send()

    @pl.loop(1, 8)
    def _(r):
        wy_copy(r).wait_send()
        for k in range(2):
            wz_copy(r, k).wait_send()

    part_ref[...] = total_of(g_z, gz)


def on_device(
    queries,
    keys_local,
    values_local,
    mem_keys,
    mem_values,
    prev_keys,
    prev_values,
    gate_logit,
    cotangent,
    block_home,
    query_blocks,
    write_slots,
):
    tables = codes(block_home, query_blocks, write_slots)
    sigmoid_gate = jax.nn.sigmoid(gate_logit)
    smem, vmem = (pl.BlockSpec(memory_space=space) for space in (pltpu.SMEM, pltpu.VMEM))
    dma = pltpu.SemaphoreType.DMA
    mixed, new_keys, new_values, part = pl.pallas_call(
        kernel,
        out_shape=(
            jax.ShapeDtypeStruct((128, 2048), BF16),
            jax.ShapeDtypeStruct((64, 128, 128), BF16),
            jax.ShapeDtypeStruct((64, 128, 128), BF16),
            jax.ShapeDtypeStruct((16, 128), F32),
        ),
        in_specs=[smem] * 6 + [vmem] * 8,
        out_specs=(vmem,) * 4,
        scratch_shapes=[
            pltpu.VMEM((8, 8, 2, 2, 128, 128), BF16),
            pltpu.VMEM((8, 8, 2, 2, 128, 128), BF16),
            pltpu.VMEM((8, 16, 128, 128), BF16),
            pltpu.VMEM((16, 128, 128), F32),
            pltpu.VMEM((16, 128, 128), F32),
            pltpu.VMEM((16, 128, 128), F32),
            pltpu.VMEM((7, 16, 128, 128), BF16),
            pltpu.VMEM((7, 128, 128), F32),
            pltpu.VMEM((7, 16, 128, 128), BF16),
            pltpu.VMEM((7, 128, 128), F32),
            pltpu.VMEM((4, 8, 2, 128, 128), BF16),
            pltpu.VMEM((8, 2, 2, 128, 128), BF16),
            pltpu.VMEM((2, 4, 2, 2, 128, 128), BF16),
            pltpu.VMEM((4, 8, 2, 2, 128, 128), BF16),
            pltpu.VMEM((16, 128), F32),
            pltpu.VMEM((ND, 16, 128), F32),
            pltpu.VMEM((NL, 16, 128), F32),
            pltpu.VMEM((NZ, 16, 128), F32),
            dma((8, 8)),
            dma((8, 8)),
            dma((2, 4)),
            dma((2, 4)),
            dma((7,)),
            dma((7,)),
            dma((7,)),
            dma((7,)),
            dma((4,)),
            dma((4,)),
            dma((8, 2)),
            dma((8, 2)),
            dma((8,)),
            dma((8,)),
            dma((4,)),
            dma((4,)),
            dma((ND,)),
            dma((ND,)),
            dma((NL,)),
            dma((NL,)),
            dma((NZ,)),
            dma((NZ,)),
        ],
        compiler_params=pltpu.CompilerParams(
            collective_id=0, has_side_effects=True, vmem_limit_bytes=60 * 1024 * 1024
        ),
    )(
        *tables,
        sigmoid_gate,
        queries,
        keys_local,
        values_local,
        cotangent,
        mem_keys.reshape(64, 128, 128),
        mem_values.reshape(64, 128, 128),
        prev_keys,
        prev_values,
    )
    total = jnp.sum(part, axis=1)
    gate_grad = sigmoid_gate * (1.0 - sigmoid_gate) * total
    return mixed, new_keys.reshape(mem_keys.shape), new_values.reshape(mem_values.shape), gate_grad


def solution(mesh):
    tokens, slabs = P(("dp", "mem"), None), P("mem", None, None, None)
    units = P(("dp", "mem"), None, None)
    return jax.shard_map(
        on_device,
        mesh=mesh,
        in_specs=(
            tokens,
            tokens,
            tokens,
            slabs,
            slabs,
            units,
            units,
            P(),
            tokens,
            P(),
            units,
            P(("dp", "mem")),
        ),
        out_specs=(tokens, slabs, slabs, P()),
        check_vma=False,
    )
```

```python
import functools
import math

import jax
import jax.numpy as jnp
from jax import lax
from jax.experimental import pallas as pl
from jax.experimental.pallas import tpu as pltpu
from jax.sharding import PartitionSpec as P

MESH = pl.DeviceIdType.MESH
BF16, F32 = jnp.bfloat16, jnp.float32
NZ, NL, ND = 8, 8, 4
OFFSETS = (3, -4, 2, -3, 1, -2, -1, 0)
NONE = -1e30
CHUNKS = 4
PART = 16 // CHUNKS
UNITS_AFTER, WY_AFTER, WX_AFTER = 1, -1, 2
FIRST = 5


def wrap(value, size):
    return lax.rem(value + 4 * size, size)


def peers(group, layer, lane):
    in_layer = lambda r: (group, layer * NL + wrap(lane + r, NL))
    along_z = lambda r: (group, wrap(layer + r, NZ) * NL + lane)
    in_groups = lambda r: (wrap(group + r, ND), layer * NL + lane)
    return in_layer, along_z, in_groups


def greet(group, layer, lane):
    barrier = pltpu.get_barrier_semaphore()
    in_layer, along_z, in_groups = peers(group, layer, lane)

    @pl.loop(1, 8)
    def _(r):
        pl.semaphore_signal(barrier, inc=1, device_id=in_layer(r), device_id_type=MESH)
        pl.semaphore_signal(barrier, inc=1, device_id=along_z(r), device_id_type=MESH)

    @pl.loop(1, 4)
    def _(r):
        pl.semaphore_signal(barrier, inc=1, device_id=in_groups(r), device_id_type=MESH)

    return lambda: pl.semaphore_wait(barrier, 17)


def remote(src, dst, s, r, to):
    return pltpu.make_async_remote_copy(
        src_ref=src, dst_ref=dst, send_sem=s, recv_sem=r, device_id=to, device_id_type=MESH
    )


def codes(block_home, query_blocks, write_slots):
    place = lax.axis_index("mem")
    lanes = jnp.arange(256, dtype=jnp.int32)
    wanted = query_blocks.reshape(16, 4)
    storage = jnp.sum(
        jnp.where(wanted[:, :, None] == lanes, block_home[:, None, :], 0), axis=-1
    ).reshape(64)
    owner = storage // 4
    count = jnp.arange(64, dtype=jnp.int32)
    rank = jnp.sum(
        ((owner[:, None] == owner[None, :]) & (count[:, None] > count[None, :])).astype(jnp.int32),
        axis=1,
    )
    homes = lax.dynamic_slice_in_dim(block_home, (place % 2) * 8, 8, 0)
    written = jnp.sum(jnp.where(write_slots[:, None] == lanes, homes, 0), axis=-1)
    packed = jnp.concatenate([storage * 2 + rank, written, jnp.zeros((56,), jnp.int32)])
    return packed.reshape(1, 128)


def kernel(
    gate,
    own,
    q_ref,
    kl_ref,
    vl_ref,
    cot_ref,
    mk_ref,
    mv_ref,
    pk_ref,
    pv_ref,
    mixed_ref,
    nk_ref,
    nv_ref,
    part_ref,
    code_all,
    rows,
    ask_v,
    ask,
    put_v,
    put,
    unit_all,
    kv_out,
    kv_in,
    q_all,
    cot_t,
    slot_o,
    slot_s,
    near_o,
    res_o,
    res_s,
    got_o,
    got_s,
    w_out,
    w_mid,
    w_in,
    part,
    g_x,
    g_l,
    g_z,
    c_send,
    c_recv,
    table_sem,
    x_send,
    x_recv,
    kv_send,
    kv_recv,
    q_send,
    q_recv,
    ro_send,
    ro_recv,
    rs_send,
    rs_recv,
    wz_send,
    wz_recv,
    wy_send,
    wy_recv,
    wx_send,
    wx_recv,
    gx_send,
    gx_recv,
    gl_send,
    gl_recv,
    gz_send,
    gz_recv,
):
    group, place = lax.axis_index("dp"), lax.axis_index("mem")
    layer, lane = lax.div(place, NL), lax.rem(place, NL)
    row = lax.div(lane, 2)
    scale = 1.0 / math.sqrt(128.0)

    def at(g, z, l):
        return (g, z * NL + l)

    ready = greet(group, layer, lane)
    in_layer, along_z, in_groups = peers(group, layer, lane)
    code_all[group, lane, layer] = own[...]
    for h in range(16):
        q_all[layer, h] = q_ref[:, h * 128 : (h + 1) * 128]
    for u in range(8):
        unit_all[group, u, 0] = pk_ref[u]
        unit_all[group, u, 1] = pv_ref[u]
    ready()

    def code_copies(step):
        part, to, size = (
            (code_all.at[group, lane, layer], along_z, NZ),
            (code_all.at[group, lane], in_layer, NL),
            (code_all.at[group], in_groups, ND),
        )[step]
        return [
            remote(part, part, c_send.at[step, k], c_recv.at[step, k], to(k))
            for k in range(1, size)
        ]

    def start_all(copies):
        for copy in copies:
            copy.start()

    def wait_all(copies):
        for copy in copies:
            copy.wait()

    start_all(code_copies(0))

    def q_copy(hop, up):
        source = wrap(layer - hop if up else layer + hop, NZ)
        to = at(group, wrap(layer + (1 if up else -1), NZ), lane)
        k = 0 if up else 1
        return remote(
            q_all.at[source], q_all.at[source], q_send.at[k, hop], q_recv.at[k, hop], to
        )

    q_copy(0, True).start()
    q_copy(0, False).start()

    def x_copy(r):
        return remote(
            unit_all.at[group], unit_all.at[group], x_send.at[r], x_recv.at[r], in_groups(r)
        )

    rows_at = lax.broadcasted_iota(jnp.int32, (128, 128), 0)
    cols_at = lax.broadcasted_iota(jnp.int32, (128, 128), 1)
    rows[...] = jnp.zeros_like(rows)
    wait_all(code_copies(0))
    start_all(code_copies(1))
    wait_all(code_copies(1))
    start_all(code_copies(2))

    @pl.loop(1, 4)
    def _(r):
        x_copy(r).start()

    def lay_rows(g):
        @pl.loop(0, NL)
        def _(l):
            for z in range(NZ):
                rows[g, pl.ds(l * NZ + z, 1), :] = code_all[g, l, z]

    def to_scalars(source, target, k):
        copy = pltpu.make_async_copy(source, target, table_sem.at[k])
        copy.start()
        copy.wait()

    def most(allowed, value, none):
        return jnp.max(jnp.where(allowed, value, none), axis=0, keepdims=True)

    lay_rows(group)
    asked = rows[group].T
    real = rows_at < 64
    for k in range(2):
        ask_v[k : k + 1, :] = most(
            real & ((asked >> 3) == place) & ((asked & 1) == k),
            ((asked >> 1) & 3) * 16 + (rows_at >> 2),
            0,
        )
    for k in range(2, 8):
        ask_v[k : k + 1, :] = jnp.zeros((1, 128), jnp.int32)
    mine = rows[group, pl.ds(pl.multiple_of(lane * NZ, NZ), NZ), :]
    ask_v[8:16, :] = jnp.where((mine >> 6) == layer, ((mine >> 3) & 7) * 2 + (mine & 1), -1)
    spots = jnp.where(real & ((asked >> 6) == layer), ((asked >> 3) & 7) * 2 + (asked & 1), -1)
    for k in range(16):
        ask_v[16 + k : 17 + k, :] = most(spots == k, rows_at >> 2, 0)
    to_scalars(ask_v, ask, 0)

    def select(tile, l, k):
        return ask[k, l * NZ + tile]

    def unit_tables():
        wait_all(code_copies(2))
        unit_at, col = rows_at[:8], cols_at[:8]
        to = (col >> 1) * NL + ((row + group + layer) & 3) * 2 + (col & 1)
        come = jnp.full((1, 128), -1, jnp.int32)
        chosen = jnp.zeros((1, 128), jnp.int32)
        for g in range(ND):
            lay_rows(g)
            places = rows[g].T[64:72, :]
            head = ((col >> 3) & 1) * 8 + unit_at
            come = jnp.maximum(
                come, most((col < 64) & ((places >> 2) == place), (places & 3) * 16 + head, -1)
            )
            column = jnp.sum(
                jnp.where(col == lane * NZ + layer, places, 0), axis=1, keepdims=True
            )
            chosen = jnp.maximum(chosen, most((column >> 2) == to, g * 8 + unit_at, 0))
        from_z, from_l = rows_at & 7, rows_at >> 3
        via = (row - (from_l >> 1) - from_z + 16) & 3
        landing = (via * NL + from_l) * 2 + (from_z >> 2)
        came = jnp.broadcast_to(come, (128, 128)).T
        put_v[...] = jnp.zeros_like(put_v)
        put_v[0:1, :] = chosen
        put_v[1:2, :] = most(came == cols_at, landing, -1)
        to_scalars(put_v, put, 1)

    def kv_copy(i, r):
        return remote(
            kv_out.at[i, r],
            kv_in.at[i, lane],
            kv_send.at[i, r],
            kv_recv.at[i, r],
            at(group, layer, wrap(lane + r, NL)),
        )

    def kv_issue(i):
        tile = wrap(layer + OFFSETS[i], NZ)
        for k in range(2):
            code = select(tile, lane, k)
            kv_in[i, lane, 0, k] = mk_ref[code]
            kv_in[i, lane, 1, k] = mv_ref[code]

        @pl.loop(1, 8)
        def _(r):
            for k in range(2):
                code = select(tile, wrap(lane + r, NL), k)
                kv_out[i, r, 0, k] = mk_ref[code]
                kv_out[i, r, 1, k] = mv_ref[code]
            kv_copy(i, r).start()

    for i in range(FIRST):
        kv_issue(i)

    def wz_copy(r, k):
        return remote(
            w_out.at[r, k],
            w_mid.at[k, lax.rem(layer, 4), lax.div(layer, 4)],
            wz_send.at[r, k],
            wz_recv.at[r, k],
            at(group, wrap(layer + r, NZ), lane),
        )

    def send_units():
        @pl.loop(1, 4)
        def _(r):
            x_copy(r).wait_recv()

        for r in range(8):
            to_layer = wrap(layer + r, NZ)
            for k in range(2):
                unit = put[0, to_layer * 2 + k]
                for kv in range(2):
                    slab = unit_all[unit // 8, unit % 8, kv]
                    if r == 0:
                        w_mid[k, lax.rem(layer, 4), lax.div(layer, 4), kv] = slab
                    else:
                        w_out[r, k, kv] = slab
                if r > 0:
                    wz_copy(r, k).start()

    def attend(qh, kh, vt, allowed=None):
        scores = (
            lax.dot_general(kh, qh, (((1,), (1,)), ((), ())), preferred_element_type=F32) * scale
        )
        if allowed is not None:
            scores = jnp.where(allowed, scores, NONE)
        top = jnp.max(scores, axis=0, keepdims=True)
        shifted = jnp.exp(scores - top)
        total = jnp.sum(shifted, axis=0, keepdims=True)
        out = jnp.dot(vt, shifted.astype(BF16), preferred_element_type=F32) * (1.0 / total)
        return out, top + jnp.log(total)

    def near(first):
        for h in range(first, first + 8):
            cols = slice(h * 128, h * 128 + 128)
            near_o[h], _ = attend(
                q_ref[:, cols], kl_ref[:, cols], vl_ref[:, cols].T, rows_at <= cols_at
            )
            cot_t[h] = cot_ref[:, cols].T

    unit_tables()
    for hop in range(4):
        q_copy(hop, True).wait_recv()
        if hop < 3:
            q_copy(hop + 1, True).start()
            q_copy(hop, False).wait_recv()
        if hop < 2:
            q_copy(hop + 1, False).start()
        if hop == UNITS_AFTER:
            send_units()
        if hop in (0, 1):
            near(8 * hop)

    def wy_copy(r):
        peer = wrap(lane + r, NL)
        low = wrap(lax.div(peer, 2) - row - group, 4)
        return remote(
            w_mid.at[lax.rem(peer, 2), low],
            w_in.at[group, lane],
            wy_send.at[r],
            wy_recv.at[r],
            at(group, layer, peer),
        )

    def wx_copy(r):
        return remote(
            w_in.at[group],
            w_in.at[group],
            wx_send.at[r],
            wx_recv.at[r],
            at(wrap(group + r, ND), layer, lane),
        )

    def result_copies(i, c):
        to = at(group, wrap(layer + (1 if OFFSETS[i] > 0 else -1), NZ), lane)
        return (
            remote(res_o.at[i, c], got_o.at[i, c], ro_send.at[i, c], ro_recv.at[i, c], to),
            remote(res_s.at[i, c], got_s.at[i, c], rs_send.at[i, c], rs_recv.at[i, c], to),
        )

    def pass_units():
        @pl.loop(1, 8)
        def _(r):
            for k in range(2):
                wz_copy(r, k).wait_recv()

        low = wrap(-group, 4)
        w_in[group, lane] = w_mid[lax.rem(lane, 2), low]

        @pl.loop(1, 8)
        def _(r):
            wy_copy(r).start()

        for k in range(FIRST, 8):
            kv_issue(k)

    if WY_AFTER < 0:
        pass_units()
    joins = []
    for i, off in enumerate(OFFSETS):
        if off == 0:
            joins.append((OFFSETS.index(1), OFFSETS.index(-1)))
        else:
            further = off + (1 if off > 0 else -1)
            joins.append((OFFSETS.index(further),) if further in OFFSETS else ())

    for i, off in enumerate(OFFSETS):
        tile = wrap(layer + off, NZ)

        @pl.loop(1, 8)
        def _(r):
            kv_copy(i, r).wait_recv()

        @pl.loop(0, 4)
        def _(step):
            for k in range(4):
                s = step * 4 + k
                head = ask[16 + s, lane * NZ + tile]
                kh, vh = kv_in[i, step * 2 + k // 2, 0, k % 2], kv_in[i, step * 2 + k // 2, 1, k % 2]
                out, stat = attend(q_all[tile, head], kh, vh.T)
                slot_o[s] = out
                slot_s[s] = stat

        for c in range(CHUNKS):
            for j in joins[i]:
                for copy in result_copies(j, c):
                    copy.wait_recv()

            @pl.loop(0, PART)
            def _(n):
                h = c * PART + n
                outs, stats = [], []
                for j in range(4):
                    where = ask[8 + tile, h * 4 + j]
                    spot = jnp.maximum(where, 0)
                    outs.append(slot_o[spot])
                    stats.append(jnp.where(where >= 0, slot_s[spot], NONE))
                for j in joins[i]:
                    outs.append(got_o[j, c, n].astype(F32))
                    stats.append(got_s[j, c, pl.ds(n, 1), :])
                top = functools.reduce(jnp.maximum, stats)
                weights = [jnp.exp(stat - top) for stat in stats]
                total = functools.reduce(jnp.add, weights)
                inverse = 1.0 / total
                out = functools.reduce(
                    jnp.add, [(w * inverse) * o for w, o in zip(weights, outs)]
                )
                if off != 0:
                    res_o[i, c, n] = out.astype(BF16)
                    res_s[i, c, pl.ds(n, 1), :] = top + jnp.log(total)
                else:
                    cols = pl.ds(pl.multiple_of(h * 128, 128), 128)
                    opening = gate[h]
                    local = near_o[h]
                    mixed_ref[:, cols] = (opening * out + (1.0 - opening) * local).T.astype(BF16)
                    part[pl.ds(h, 1), :] = jnp.sum(
                        cot_t[h].astype(F32) * (out - local), axis=0, keepdims=True
                    )

            if off != 0:
                for copy in result_copies(i, c):
                    copy.start()

        if i == WY_AFTER:
            pass_units()

        if i == WX_AFTER:
            @pl.loop(1, 8)
            def _(r):
                wy_copy(r).wait_recv()

            @pl.loop(1, 4)
            def _(r):
                wx_copy(r).start()


    def spread(value, held, mine, size, s, r, to):
        held[mine] = value
        copies = [
            remote(held.at[mine], held.at[mine], s.at[k], r.at[k], to(k)) for k in range(1, size)
        ]
        for copy in copies:
            copy.start()
        return copies

    def total_of(held, copies):
        for copy in copies:
            copy.wait()
        return jnp.sum(held[...], axis=0)

    gx = spread(part[...], g_x, group, ND, gx_send, gx_recv, in_groups)

    @pl.loop(1, 4)
    def _(r):
        wx_copy(r).wait_recv()

    gl = spread(total_of(g_x, gx), g_l, lane, NL, gl_send, gl_recv, in_layer)

    @pl.loop(0, 64)
    def _(slab):
        where = put[1, slab]
        spot = jnp.maximum(where, 0)
        for kv, (old, new) in enumerate(((mk_ref, nk_ref), (mv_ref, nv_ref))):
            came = w_in[spot // 16, spot // 2 % 8, spot % 2, kv]
            new[slab] = jnp.where(where >= 0, came, old[slab])

    gz = spread(total_of(g_l, gl), g_z, layer, NZ, gz_send, gz_recv, along_z)

    for hop in range(4):
        q_copy(hop, True).wait_send()
        if hop < 3:
            q_copy(hop, False).wait_send()
    for i, off in enumerate(OFFSETS):
        if off != 0:
            for c in range(CHUNKS):
                for copy in result_copies(i, c):
                    copy.wait_send()

        @pl.loop(1, 8)
        def _(r):
            kv_copy(i, r).wait_send()

    @pl.loop(1, 4)
    def _(r):
        x_copy(r).wait_send()
        wx_copy(r).wait_send()

    @pl.loop(1, 8)
    def _(r):
        wy_copy(r).wait_send()
        for k in range(2):
            wz_copy(r, k).wait_send()

    part_ref[...] = total_of(g_z, gz)


def on_device(
    queries,
    keys_local,
    values_local,
    mem_keys,
    mem_values,
    prev_keys,
    prev_values,
    gate_logit,
    cotangent,
    block_home,
    query_blocks,
    write_slots,
):
    own = codes(block_home, query_blocks, write_slots)
    sigmoid_gate = jax.nn.sigmoid(gate_logit)
    smem, vmem = (pl.BlockSpec(memory_space=space) for space in (pltpu.SMEM, pltpu.VMEM))
    dma = pltpu.SemaphoreType.DMA
    mixed, new_keys, new_values, part = pl.pallas_call(
        kernel,
        out_shape=(
            jax.ShapeDtypeStruct((128, 2048), BF16),
            jax.ShapeDtypeStruct((64, 128, 128), BF16),
            jax.ShapeDtypeStruct((64, 128, 128), BF16),
            jax.ShapeDtypeStruct((16, 128), F32),
        ),
        in_specs=[smem] + [vmem] * 9,
        out_specs=(vmem,) * 4,
        scratch_shapes=[
            pltpu.VMEM((ND, NL, NZ, 1, 128), jnp.int32),
            pltpu.VMEM((ND, 128, 128), jnp.int32),
            pltpu.VMEM((32, 128), jnp.int32),
            pltpu.SMEM((32, 128), jnp.int32),
            pltpu.VMEM((8, 128), jnp.int32),
            pltpu.SMEM((8, 128), jnp.int32),
            pltpu.VMEM((ND, 8, 2, 128, 128), BF16),
            pltpu.VMEM((8, 8, 2, 2, 128, 128), BF16),
            pltpu.VMEM((8, 8, 2, 2, 128, 128), BF16),
            pltpu.VMEM((8, 16, 128, 128), BF16),
            pltpu.VMEM((16, 128, 128), BF16),
            pltpu.VMEM((16, 128, 128), F32),
            pltpu.VMEM((16, 1, 128), F32),
            pltpu.VMEM((16, 128, 128), F32),
            pltpu.VMEM((7, CHUNKS, PART, 128, 128), BF16),
            pltpu.VMEM((7, CHUNKS, PART, 128), F32),
            pltpu.VMEM((7, CHUNKS, PART, 128, 128), BF16),
            pltpu.VMEM((7, CHUNKS, PART, 128), F32),
            pltpu.VMEM((8, 2, 2, 128, 128), BF16),
            pltpu.VMEM((2, 4, 2, 2, 128, 128), BF16),
            pltpu.VMEM((4, 8, 2, 2, 128, 128), BF16),
            pltpu.VMEM((16, 128), F32),
            pltpu.VMEM((ND, 16, 128), F32),
            pltpu.VMEM((NL, 16, 128), F32),
            pltpu.VMEM((NZ, 16, 128), F32),
            dma((3, 8)),
            dma((3, 8)),
            dma((2,)),
            dma((ND,)),
            dma((ND,)),
            dma((8, 8)),
            dma((8, 8)),
            dma((2, 4)),
            dma((2, 4)),
            dma((7, CHUNKS)),
            dma((7, CHUNKS)),
            dma((7, CHUNKS)),
            dma((7, CHUNKS)),
            dma((8, 2)),
            dma((8, 2)),
            dma((8,)),
            dma((8,)),
            dma((4,)),
            dma((4,)),
            dma((ND,)),
            dma((ND,)),
            dma((NL,)),
            dma((NL,)),
            dma((NZ,)),
            dma((NZ,)),
        ],
        compiler_params=pltpu.CompilerParams(
            collective_id=0, has_side_effects=True, vmem_limit_bytes=60 * 1024 * 1024
        ),
    )(
        sigmoid_gate,
        own,
        queries,
        keys_local,
        values_local,
        cotangent,
        mem_keys.reshape(64, 128, 128),
        mem_values.reshape(64, 128, 128),
        prev_keys,
        prev_values,
    )
    total = jnp.sum(part, axis=1)
    gate_grad = sigmoid_gate * (1.0 - sigmoid_gate) * total
    return mixed, new_keys.reshape(mem_keys.shape), new_values.reshape(mem_values.shape), gate_grad


def solution(mesh):
    tokens, slabs = P(("dp", "mem"), None), P("mem", None, None, None)
    units = P(("dp", "mem"), None, None)
    return jax.shard_map(
        on_device,
        mesh=mesh,
        in_specs=(
            tokens,
            tokens,
            tokens,
            slabs,
            slabs,
            units,
            units,
            P(),
            tokens,
            P(),
            units,
            P(("dp", "mem")),
        ),
        out_specs=(tokens, slabs, slabs, P()),
        check_vma=False,
    )
```

```python
import functools
import math

import jax
import jax.numpy as jnp
from jax import lax
from jax.experimental import pallas as pl
from jax.experimental.pallas import tpu as pltpu
from jax.sharding import PartitionSpec as P

MESH = pl.DeviceIdType.MESH
BF16, F32 = jnp.bfloat16, jnp.float32
NZ, NL, ND = 8, 8, 4
OFFSETS = (-4, 3, -3, 2, -2, 1, -1, 0)
NONE = -1e30
CHUNKS = 4
PART = 16 // CHUNKS
UNITS_AFTER, WY_AFTER, WX_AFTER = 1, -1, 2
FIRST = 5


def wrap(value, size):
    return lax.rem(value + 4 * size, size)


def peers(group, layer, lane):
    in_layer = lambda r: (group, layer * NL + wrap(lane + r, NL))
    along_z = lambda r: (group, wrap(layer + r, NZ) * NL + lane)
    in_groups = lambda r: (wrap(group + r, ND), layer * NL + lane)
    return in_layer, along_z, in_groups


def greet(group, layer, lane):
    barrier = pltpu.get_barrier_semaphore()
    in_layer, along_z, in_groups = peers(group, layer, lane)

    @pl.loop(1, 8)
    def _(r):
        pl.semaphore_signal(barrier, inc=1, device_id=in_layer(r), device_id_type=MESH)
        pl.semaphore_signal(barrier, inc=1, device_id=along_z(r), device_id_type=MESH)

    @pl.loop(1, 4)
    def _(r):
        pl.semaphore_signal(barrier, inc=1, device_id=in_groups(r), device_id_type=MESH)

    return lambda: pl.semaphore_wait(barrier, 17)


def remote(src, dst, s, r, to):
    return pltpu.make_async_remote_copy(
        src_ref=src, dst_ref=dst, send_sem=s, recv_sem=r, device_id=to, device_id_type=MESH
    )


def codes(block_home, query_blocks, write_slots):
    place = lax.axis_index("mem")
    lanes = jnp.arange(256, dtype=jnp.int32)
    wanted = query_blocks.reshape(16, 4)
    storage = jnp.sum(
        jnp.where(wanted[:, :, None] == lanes, block_home[:, None, :], 0), axis=-1
    ).reshape(64)
    owner = storage // 4
    count = jnp.arange(64, dtype=jnp.int32)
    rank = jnp.sum(
        ((owner[:, None] == owner[None, :]) & (count[:, None] > count[None, :])).astype(jnp.int32),
        axis=1,
    )
    homes = lax.dynamic_slice_in_dim(block_home, (place % 2) * 8, 8, 0)
    written = jnp.sum(jnp.where(write_slots[:, None] == lanes, homes, 0), axis=-1)
    packed = jnp.concatenate([storage * 2 + rank, written, jnp.zeros((56,), jnp.int32)])
    return packed.reshape(1, 128)


def kernel(
    gate,
    own,
    q_ref,
    kl_hbm,
    vl_hbm,
    cot_hbm,
    mk_hbm,
    mv_hbm,
    pk_ref,
    pv_ref,
    mixed_ref,
    nk_ref,
    nv_ref,
    part_ref,
    kl_ref,
    vl_ref,
    cot_ref,
    mk_ref,
    mv_ref,
    code_all,
    rows,
    ask_v,
    ask,
    put_v,
    put,
    unit_all,
    kv_out,
    kv_in,
    q_all,
    cot_t,
    slot_o,
    slot_s,
    near_o,
    res_o,
    res_s,
    got_o,
    got_s,
    w_out,
    w_mid,
    w_in,
    part,
    g_x,
    g_l,
    g_z,
    load_sem,
    c_send,
    c_recv,
    table_sem,
    x_send,
    x_recv,
    kv_send,
    kv_recv,
    q_send,
    q_recv,
    ro_send,
    ro_recv,
    rs_send,
    rs_recv,
    wz_send,
    wz_recv,
    wy_send,
    wy_recv,
    wx_send,
    wx_recv,
    gx_send,
    gx_recv,
    gl_send,
    gl_recv,
    gz_send,
    gz_recv,
):
    group, place = lax.axis_index("dp"), lax.axis_index("mem")
    layer, lane = lax.div(place, NL), lax.rem(place, NL)
    row = lax.div(lane, 2)
    scale = 1.0 / math.sqrt(128.0)

    def at(g, z, l):
        return (g, z * NL + l)

    ready = greet(group, layer, lane)
    in_layer, along_z, in_groups = peers(group, layer, lane)
    loads = [
        pltpu.make_async_copy(source, target, load_sem.at[k])
        for k, (source, target) in enumerate(
            (
                (mk_hbm, mk_ref),
                (mv_hbm, mv_ref),
                (kl_hbm, kl_ref),
                (vl_hbm, vl_ref),
                (cot_hbm, cot_ref),
            )
        )
    ]
    for load in loads:
        load.start()
    code_all[group, lane, layer] = own[...]
    for h in range(16):
        q_all[layer, h] = q_ref[:, h * 128 : (h + 1) * 128]
    for u in range(8):
        unit_all[group, u, 0] = pk_ref[u]
        unit_all[group, u, 1] = pv_ref[u]
    ready()

    def code_copies(step):
        part, to, size = (
            (code_all.at[group, lane, layer], along_z, NZ),
            (code_all.at[group, lane], in_layer, NL),
            (code_all.at[group], in_groups, ND),
        )[step]
        return [
            remote(part, part, c_send.at[step, k], c_recv.at[step, k], to(k))
            for k in range(1, size)
        ]

    def start_all(copies):
        for copy in copies:
            copy.start()

    def wait_all(copies):
        for copy in copies:
            copy.wait()

    start_all(code_copies(0))

    def q_copy(hop, up):
        source = wrap(layer - hop if up else layer + hop, NZ)
        to = at(group, wrap(layer + (1 if up else -1), NZ), lane)
        k = 0 if up else 1
        part = q_all.at[source, pl.ds(8 * k, 8)] if hop == 3 else q_all.at[source]
        return remote(part, part, q_send.at[k, hop], q_recv.at[k, hop], to)

    q_copy(0, True).start()
    q_copy(0, False).start()

    def x_copy(r):
        return remote(
            unit_all.at[group], unit_all.at[group], x_send.at[r], x_recv.at[r], in_groups(r)
        )

    rows_at = lax.broadcasted_iota(jnp.int32, (128, 128), 0)
    cols_at = lax.broadcasted_iota(jnp.int32, (128, 128), 1)
    rows[...] = jnp.zeros_like(rows)
    wait_all(code_copies(0))
    start_all(code_copies(1))
    wait_all(code_copies(1))
    start_all(code_copies(2))

    @pl.loop(1, 4)
    def _(r):
        x_copy(r).start()

    def lay_rows(g):
        @pl.loop(0, NL)
        def _(l):
            for z in range(NZ):
                rows[g, pl.ds(l * NZ + z, 1), :] = code_all[g, l, z]

    def to_scalars(source, target, k):
        copy = pltpu.make_async_copy(source, target, table_sem.at[k])
        copy.start()
        copy.wait()

    def most(allowed, value, none):
        return jnp.max(jnp.where(allowed, value, none), axis=0, keepdims=True)

    lay_rows(group)
    asked = rows[group].T
    real = rows_at < 64
    for k in range(2):
        ask_v[k : k + 1, :] = most(
            real & ((asked >> 3) == place) & ((asked & 1) == k),
            ((asked >> 1) & 3) * 16 + (rows_at >> 2),
            0,
        )
    for k in range(2, 8):
        ask_v[k : k + 1, :] = jnp.zeros((1, 128), jnp.int32)
    mine = rows[group, pl.ds(pl.multiple_of(lane * NZ, NZ), NZ), :]
    ask_v[8:16, :] = jnp.where((mine >> 6) == layer, ((mine >> 3) & 7) * 2 + (mine & 1), -1)
    spots = jnp.where(real & ((asked >> 6) == layer), ((asked >> 3) & 7) * 2 + (asked & 1), -1)
    for k in range(16):
        ask_v[16 + k : 17 + k, :] = most(spots == k, rows_at >> 2, 0)
    to_scalars(ask_v, ask, 0)

    def select(tile, l, k):
        return ask[k, l * NZ + tile]

    def unit_tables():
        wait_all(code_copies(2))
        unit_at, col = rows_at[:8], cols_at[:8]
        to = (col >> 1) * NL + ((row + group + layer) & 3) * 2 + (col & 1)
        come = jnp.full((1, 128), -1, jnp.int32)
        chosen = jnp.zeros((1, 128), jnp.int32)
        for g in range(ND):
            lay_rows(g)
            places = rows[g].T[64:72, :]
            head = ((col >> 3) & 1) * 8 + unit_at
            come = jnp.maximum(
                come, most((col < 64) & ((places >> 2) == place), (places & 3) * 16 + head, -1)
            )
            column = jnp.sum(
                jnp.where(col == lane * NZ + layer, places, 0), axis=1, keepdims=True
            )
            chosen = jnp.maximum(chosen, most((column >> 2) == to, g * 8 + unit_at, 0))
        from_z, from_l = rows_at & 7, rows_at >> 3
        via = (row - (from_l >> 1) - from_z + 16) & 3
        landing = (via * NL + from_l) * 2 + (from_z >> 2)
        came = jnp.broadcast_to(come, (128, 128)).T
        put_v[...] = jnp.zeros_like(put_v)
        put_v[0:1, :] = chosen
        put_v[1:2, :] = most(came == cols_at, landing, -1)
        to_scalars(put_v, put, 1)

    def kv_copy(i, r):
        return remote(
            kv_out.at[i, r],
            kv_in.at[i, lane],
            kv_send.at[i, r],
            kv_recv.at[i, r],
            at(group, layer, wrap(lane + r, NL)),
        )

    def kv_issue(i):
        tile = wrap(layer + OFFSETS[i], NZ)
        for k in range(2):
            code = select(tile, lane, k)
            kv_in[i, lane, 0, k] = mk_ref[code]
            kv_in[i, lane, 1, k] = mv_ref[code]

        @pl.loop(1, 8)
        def _(r):
            for k in range(2):
                code = select(tile, wrap(lane + r, NL), k)
                kv_out[i, r, 0, k] = mk_ref[code]
                kv_out[i, r, 1, k] = mv_ref[code]
            kv_copy(i, r).start()

    for load in loads:
        load.wait()
    for i in range(FIRST):
        kv_issue(i)

    def wz_copy(r, k):
        return remote(
            w_out.at[r, k],
            w_mid.at[k, lax.rem(layer, 4), lax.div(layer, 4)],
            wz_send.at[r, k],
            wz_recv.at[r, k],
            at(group, wrap(layer + r, NZ), lane),
        )

    def send_units():
        @pl.loop(1, 4)
        def _(r):
            x_copy(r).wait_recv()

        for r in range(8):
            to_layer = wrap(layer + r, NZ)
            for k in range(2):
                unit = put[0, to_layer * 2 + k]
                for kv in range(2):
                    slab = unit_all[unit // 8, unit % 8, kv]
                    if r == 0:
                        w_mid[k, lax.rem(layer, 4), lax.div(layer, 4), kv] = slab
                    else:
                        w_out[r, k, kv] = slab
                if r > 0:
                    wz_copy(r, k).start()

    def attend(qh, kh, vt, allowed=None):
        scores = (
            lax.dot_general(kh, qh, (((1,), (1,)), ((), ())), preferred_element_type=F32) * scale
        )
        if allowed is not None:
            scores = jnp.where(allowed, scores, NONE)
        top = jnp.max(scores, axis=0, keepdims=True)
        shifted = jnp.exp(scores - top)
        total = jnp.sum(shifted, axis=0, keepdims=True)
        out = jnp.dot(vt, shifted.astype(BF16), preferred_element_type=F32) * (1.0 / total)
        return out, top + jnp.log(total)

    def near(first):
        for h in range(first, first + 8):
            cols = slice(h * 128, h * 128 + 128)
            near_o[h], _ = attend(
                q_ref[:, cols], kl_ref[:, cols], vl_ref[:, cols].T, rows_at <= cols_at
            )
            cot_t[h] = cot_ref[:, cols].T

    unit_tables()
    for hop in range(4):
        q_copy(hop, True).wait_recv()
        if hop < 3:
            q_copy(hop + 1, True).start()
        q_copy(hop, False).wait_recv()
        if hop < 3:
            q_copy(hop + 1, False).start()
        if hop == UNITS_AFTER:
            send_units()
        if hop in (0, 1):
            near(8 * hop)

    def wy_copy(r):
        peer = wrap(lane + r, NL)
        low = wrap(lax.div(peer, 2) - row - group, 4)
        return remote(
            w_mid.at[lax.rem(peer, 2), low],
            w_in.at[group, lane],
            wy_send.at[r],
            wy_recv.at[r],
            at(group, layer, peer),
        )

    def wx_copy(r):
        return remote(
            w_in.at[group],
            w_in.at[group],
            wx_send.at[r],
            wx_recv.at[r],
            at(wrap(group + r, ND), layer, lane),
        )

    def result_copies(i, c):
        up = OFFSETS[i] > 0 or (OFFSETS[i] == -4 and c >= CHUNKS // 2)
        to = at(group, wrap(layer + (1 if up else -1), NZ), lane)
        return (
            remote(res_o.at[i, c], got_o.at[i, c], ro_send.at[i, c], ro_recv.at[i, c], to),
            remote(res_s.at[i, c], got_s.at[i, c], rs_send.at[i, c], rs_recv.at[i, c], to),
        )

    def pass_units():
        @pl.loop(1, 8)
        def _(r):
            for k in range(2):
                wz_copy(r, k).wait_recv()

        low = wrap(-group, 4)
        w_in[group, lane] = w_mid[lax.rem(lane, 2), low]

        @pl.loop(1, 8)
        def _(r):
            wy_copy(r).start()

        for k in range(FIRST, 8):
            kv_issue(k)

    if WY_AFTER < 0:
        pass_units()
    def joins(i, c):
        off = OFFSETS[i]
        if off == 0:
            return OFFSETS.index(1), OFFSETS.index(-1)
        if abs(off) == 3:
            return (0,) if (off > 0) == (c >= CHUNKS // 2) else ()
        return () if off == -4 else (OFFSETS.index(off + (1 if off > 0 else -1)),)

    for i, off in enumerate(OFFSETS):
        tile = wrap(layer + off, NZ)

        @pl.loop(1, 8)
        def _(r):
            kv_copy(i, r).wait_recv()

        @pl.loop(0, 4)
        def _(step):
            for k in range(4):
                s = step * 4 + k
                head = ask[16 + s, lane * NZ + tile]
                kh, vh = kv_in[i, step * 2 + k // 2, 0, k % 2], kv_in[i, step * 2 + k // 2, 1, k % 2]
                out, stat = attend(q_all[tile, head], kh, vh.T)
                slot_o[s] = out
                slot_s[s] = stat

        for c in range(CHUNKS):
            for j in joins(i, c):
                for copy in result_copies(j, c):
                    copy.wait_recv()

            @pl.loop(0, PART)
            def _(n):
                h = c * PART + n
                outs, stats = [], []
                for j in range(4):
                    where = ask[8 + tile, h * 4 + j]
                    spot = jnp.maximum(where, 0)
                    outs.append(slot_o[spot])
                    stats.append(jnp.where(where >= 0, slot_s[spot], NONE))
                for j in joins(i, c):
                    outs.append(got_o[j, c, n].astype(F32))
                    stats.append(got_s[j, c, pl.ds(n, 1), :])
                top = functools.reduce(jnp.maximum, stats)
                weights = [jnp.exp(stat - top) for stat in stats]
                total = functools.reduce(jnp.add, weights)
                inverse = 1.0 / total
                out = functools.reduce(
                    jnp.add, [(w * inverse) * o for w, o in zip(weights, outs)]
                )
                if off != 0:
                    res_o[i, c, n] = out.astype(BF16)
                    res_s[i, c, pl.ds(n, 1), :] = top + jnp.log(total)
                else:
                    cols = pl.ds(pl.multiple_of(h * 128, 128), 128)
                    opening = gate[h]
                    local = near_o[h]
                    mixed_ref[:, cols] = (opening * out + (1.0 - opening) * local).T.astype(BF16)
                    part[pl.ds(h, 1), :] = jnp.sum(
                        cot_t[h].astype(F32) * (out - local), axis=0, keepdims=True
                    )

            if off != 0:
                for copy in result_copies(i, c):
                    copy.start()

        if i == WY_AFTER:
            pass_units()

        if i == WX_AFTER:
            @pl.loop(1, 8)
            def _(r):
                wy_copy(r).wait_recv()

            @pl.loop(1, 4)
            def _(r):
                wx_copy(r).start()


    def spread(value, held, mine, size, s, r, to):
        held[mine] = value
        copies = [
            remote(held.at[mine], held.at[mine], s.at[k], r.at[k], to(k)) for k in range(1, size)
        ]
        for copy in copies:
            copy.start()
        return copies

    def total_of(held, copies):
        for copy in copies:
            copy.wait()
        return jnp.sum(held[...], axis=0)

    gx = spread(part[...], g_x, group, ND, gx_send, gx_recv, in_groups)

    @pl.loop(1, 4)
    def _(r):
        wx_copy(r).wait_recv()

    gl = spread(total_of(g_x, gx), g_l, lane, NL, gl_send, gl_recv, in_layer)

    @pl.loop(0, 64)
    def _(slab):
        where = put[1, slab]
        spot = jnp.maximum(where, 0)
        for kv, (old, new) in enumerate(((mk_ref, nk_ref), (mv_ref, nv_ref))):
            came = w_in[spot // 16, spot // 2 % 8, spot % 2, kv]
            new[slab] = jnp.where(where >= 0, came, old[slab])

    gz = spread(total_of(g_l, gl), g_z, layer, NZ, gz_send, gz_recv, along_z)

    for hop in range(4):
        q_copy(hop, True).wait_send()
        q_copy(hop, False).wait_send()
    for i, off in enumerate(OFFSETS):
        if off != 0:
            for c in range(CHUNKS):
                for copy in result_copies(i, c):
                    copy.wait_send()

        @pl.loop(1, 8)
        def _(r):
            kv_copy(i, r).wait_send()

    @pl.loop(1, 4)
    def _(r):
        x_copy(r).wait_send()
        wx_copy(r).wait_send()

    @pl.loop(1, 8)
    def _(r):
        wy_copy(r).wait_send()
        for k in range(2):
            wz_copy(r, k).wait_send()

    part_ref[...] = total_of(g_z, gz)


def on_device(
    queries,
    keys_local,
    values_local,
    mem_keys,
    mem_values,
    prev_keys,
    prev_values,
    gate_logit,
    cotangent,
    block_home,
    query_blocks,
    write_slots,
):
    own = codes(block_home, query_blocks, write_slots)
    sigmoid_gate = jax.nn.sigmoid(gate_logit)
    smem, vmem, later = (
        pl.BlockSpec(memory_space=space) for space in (pltpu.SMEM, pltpu.VMEM, pl.ANY)
    )
    dma = pltpu.SemaphoreType.DMA
    mixed, new_keys, new_values, part = pl.pallas_call(
        kernel,
        out_shape=(
            jax.ShapeDtypeStruct((128, 2048), BF16),
            jax.ShapeDtypeStruct((64, 128, 128), BF16),
            jax.ShapeDtypeStruct((64, 128, 128), BF16),
            jax.ShapeDtypeStruct((16, 128), F32),
        ),
        in_specs=[smem] + [vmem] * 2 + [later] * 5 + [vmem] * 2,
        out_specs=(vmem,) * 4,
        scratch_shapes=[
            pltpu.VMEM((128, 2048), BF16),
            pltpu.VMEM((128, 2048), BF16),
            pltpu.VMEM((128, 2048), BF16),
            pltpu.VMEM((64, 128, 128), BF16),
            pltpu.VMEM((64, 128, 128), BF16),
            pltpu.VMEM((ND, NL, NZ, 1, 128), jnp.int32),
            pltpu.VMEM((ND, 128, 128), jnp.int32),
            pltpu.VMEM((32, 128), jnp.int32),
            pltpu.SMEM((32, 128), jnp.int32),
            pltpu.VMEM((8, 128), jnp.int32),
            pltpu.SMEM((8, 128), jnp.int32),
            pltpu.VMEM((ND, 8, 2, 128, 128), BF16),
            pltpu.VMEM((8, 8, 2, 2, 128, 128), BF16),
            pltpu.VMEM((8, 8, 2, 2, 128, 128), BF16),
            pltpu.VMEM((8, 16, 128, 128), BF16),
            pltpu.VMEM((16, 128, 128), BF16),
            pltpu.VMEM((16, 128, 128), F32),
            pltpu.VMEM((16, 1, 128), F32),
            pltpu.VMEM((16, 128, 128), F32),
            pltpu.VMEM((7, CHUNKS, PART, 128, 128), BF16),
            pltpu.VMEM((7, CHUNKS, PART, 128), F32),
            pltpu.VMEM((7, CHUNKS, PART, 128, 128), BF16),
            pltpu.VMEM((7, CHUNKS, PART, 128), F32),
            pltpu.VMEM((8, 2, 2, 128, 128), BF16),
            pltpu.VMEM((2, 4, 2, 2, 128, 128), BF16),
            pltpu.VMEM((4, 8, 2, 2, 128, 128), BF16),
            pltpu.VMEM((16, 128), F32),
            pltpu.VMEM((ND, 16, 128), F32),
            pltpu.VMEM((NL, 16, 128), F32),
            pltpu.VMEM((NZ, 16, 128), F32),
            dma((5,)),
            dma((3, 8)),
            dma((3, 8)),
            dma((2,)),
            dma((ND,)),
            dma((ND,)),
            dma((8, 8)),
            dma((8, 8)),
            dma((2, 4)),
            dma((2, 4)),
            dma((7, CHUNKS)),
            dma((7, CHUNKS)),
            dma((7, CHUNKS)),
            dma((7, CHUNKS)),
            dma((8, 2)),
            dma((8, 2)),
            dma((8,)),
            dma((8,)),
            dma((4,)),
            dma((4,)),
            dma((ND,)),
            dma((ND,)),
            dma((NL,)),
            dma((NL,)),
            dma((NZ,)),
            dma((NZ,)),
        ],
        compiler_params=pltpu.CompilerParams(
            collective_id=0, has_side_effects=True, vmem_limit_bytes=60 * 1024 * 1024
        ),
    )(
        sigmoid_gate,
        own,
        queries,
        keys_local,
        values_local,
        cotangent,
        mem_keys.reshape(64, 128, 128),
        mem_values.reshape(64, 128, 128),
        prev_keys,
        prev_values,
    )
    total = jnp.sum(part, axis=1)
    gate_grad = sigmoid_gate * (1.0 - sigmoid_gate) * total
    return mixed, new_keys.reshape(mem_keys.shape), new_values.reshape(mem_values.shape), gate_grad


def solution(mesh):
    tokens, slabs = P(("dp", "mem"), None), P("mem", None, None, None)
    units = P(("dp", "mem"), None, None)
    return jax.shard_map(
        on_device,
        mesh=mesh,
        in_specs=(
            tokens,
            tokens,
            tokens,
            slabs,
            slabs,
            units,
            units,
            P(),
            tokens,
            P(),
            units,
            P(("dp", "mem")),
        ),
        out_specs=(tokens, slabs, slabs, P()),
        check_vma=False,
    )
```

```python
import functools
import math

import jax
import jax.numpy as jnp
from jax import lax
from jax.experimental import pallas as pl
from jax.experimental.pallas import tpu as pltpu
from jax.sharding import PartitionSpec as P

MESH = pl.DeviceIdType.MESH
BF16, F32 = jnp.bfloat16, jnp.float32
NZ, NL, ND = 8, 8, 4
OFFSETS = (-4, 3, -3, 2, -2, 1, -1, 0)
NONE = -1e30
CHUNKS = 4
PART = 16 // CHUNKS
UNITS_AFTER, WY_AFTER, WX_AFTER = 1, -1, 2
FIRST = 5


def wrap(value, size):
    return lax.rem(value + 4 * size, size)


def peers(group, layer, lane):
    in_layer = lambda r: (group, layer * NL + wrap(lane + r, NL))
    along_z = lambda r: (group, wrap(layer + r, NZ) * NL + lane)
    in_groups = lambda r: (wrap(group + r, ND), layer * NL + lane)
    return in_layer, along_z, in_groups


def greet(group, layer, lane):
    barrier = pltpu.get_barrier_semaphore()
    in_layer, along_z, in_groups = peers(group, layer, lane)

    @pl.loop(1, 8)
    def _(r):
        pl.semaphore_signal(barrier, inc=1, device_id=in_layer(r), device_id_type=MESH)
        pl.semaphore_signal(barrier, inc=1, device_id=along_z(r), device_id_type=MESH)

    @pl.loop(1, 4)
    def _(r):
        pl.semaphore_signal(barrier, inc=1, device_id=in_groups(r), device_id_type=MESH)

    return lambda: pl.semaphore_wait(barrier, 17)


def remote(src, dst, s, r, to):
    return pltpu.make_async_remote_copy(
        src_ref=src, dst_ref=dst, send_sem=s, recv_sem=r, device_id=to, device_id_type=MESH
    )


def codes(block_home, query_blocks, write_slots):
    place = lax.axis_index("mem")
    lanes = jnp.arange(256, dtype=jnp.int32)
    wanted = query_blocks.reshape(16, 4)
    storage = jnp.sum(
        jnp.where(wanted[:, :, None] == lanes, block_home[:, None, :], 0), axis=-1
    ).reshape(64)
    owner = storage // 4
    count = jnp.arange(64, dtype=jnp.int32)
    rank = jnp.sum(
        ((owner[:, None] == owner[None, :]) & (count[:, None] > count[None, :])).astype(jnp.int32),
        axis=1,
    )
    homes = lax.dynamic_slice_in_dim(block_home, (place % 2) * 8, 8, 0)
    written = jnp.sum(jnp.where(write_slots[:, None] == lanes, homes, 0), axis=-1)
    packed = jnp.concatenate([storage * 2 + rank, written, jnp.zeros((56,), jnp.int32)])
    return packed.reshape(1, 128)


def kernel(
    gate,
    own,
    q_ref,
    kl_hbm,
    vl_hbm,
    cot_hbm,
    mk_hbm,
    mv_hbm,
    pk_ref,
    pv_ref,
    mixed_ref,
    nk_ref,
    nv_ref,
    part_ref,
    kl_ref,
    vl_ref,
    cot_ref,
    mk_ref,
    mv_ref,
    code_all,
    rows,
    ask_v,
    ask,
    put_v,
    put,
    unit_all,
    kv_out,
    kv_in,
    q_all,
    cot_t,
    slot_o,
    slot_s,
    near_o,
    res_o,
    res_s,
    got_o,
    got_s,
    w_out,
    w_mid,
    w_in,
    part,
    g_x,
    g_l,
    g_z,
    load_sem,
    c_send,
    c_recv,
    table_sem,
    x_send,
    x_recv,
    kv_send,
    kv_recv,
    q_send,
    q_recv,
    ro_send,
    ro_recv,
    rs_send,
    rs_recv,
    wz_send,
    wz_recv,
    wy_send,
    wy_recv,
    wx_send,
    wx_recv,
    gx_send,
    gx_recv,
    gl_send,
    gl_recv,
    gz_send,
    gz_recv,
):
    group, place = lax.axis_index("dp"), lax.axis_index("mem")
    layer, lane = lax.div(place, NL), lax.rem(place, NL)
    row = lax.div(lane, 2)
    scale = 1.0 / math.sqrt(128.0)

    def at(g, z, l):
        return (g, z * NL + l)

    ready = greet(group, layer, lane)
    in_layer, along_z, in_groups = peers(group, layer, lane)
    loads = [
        pltpu.make_async_copy(source, target, load_sem.at[k])
        for k, (source, target) in enumerate(
            (
                (mk_hbm, mk_ref),
                (mv_hbm, mv_ref),
                (kl_hbm, kl_ref),
                (vl_hbm, vl_ref),
                (cot_hbm, cot_ref),
            )
        )
    ]
    for load in loads:
        load.start()
    code_all[group, lane, layer] = own[...]
    for h in range(16):
        q_all[layer, h] = q_ref[:, h * 128 : (h + 1) * 128]
    for u in range(8):
        unit_all[group, u, 0] = pk_ref[u]
        unit_all[group, u, 1] = pv_ref[u]
    ready()

    def code_copies(step):
        part, to, size = (
            (code_all.at[group, lane, layer], along_z, NZ),
            (code_all.at[group, lane], in_layer, NL),
            (code_all.at[group], in_groups, ND),
        )[step]
        return [
            remote(part, part, c_send.at[step, k], c_recv.at[step, k], to(k))
            for k in range(1, size)
        ]

    def start_all(copies):
        for copy in copies:
            copy.start()

    def wait_all(copies):
        for copy in copies:
            copy.wait()

    def x_copy(r):
        return remote(
            unit_all.at[group], unit_all.at[group], x_send.at[r], x_recv.at[r], in_groups(r)
        )

    start_all(code_copies(0))

    @pl.loop(1, 4)
    def _(r):
        x_copy(r).start()

    def q_copy(hop, up):
        source = wrap(layer - hop if up else layer + hop, NZ)
        to = at(group, wrap(layer + (1 if up else -1), NZ), lane)
        k = 0 if up else 1
        part = q_all.at[source, pl.ds(8 * k, 8)] if hop == 3 else q_all.at[source]
        return remote(part, part, q_send.at[k, hop], q_recv.at[k, hop], to)

    q_copy(0, True).start()
    q_copy(0, False).start()

    rows_at = lax.broadcasted_iota(jnp.int32, (128, 128), 0)
    cols_at = lax.broadcasted_iota(jnp.int32, (128, 128), 1)
    rows[...] = jnp.zeros_like(rows)
    wait_all(code_copies(0))
    start_all(code_copies(1))
    wait_all(code_copies(1))
    start_all(code_copies(2))

    def lay_rows(g):
        @pl.loop(0, NL)
        def _(l):
            for z in range(NZ):
                rows[g, pl.ds(l * NZ + z, 1), :] = code_all[g, l, z]

    def to_scalars(source, target, k):
        copy = pltpu.make_async_copy(source, target, table_sem.at[k])
        copy.start()
        copy.wait()

    def most(allowed, value, none):
        return jnp.max(jnp.where(allowed, value, none), axis=0, keepdims=True)

    lay_rows(group)
    asked = rows[group].T
    real = rows_at < 64
    for k in range(2):
        ask_v[k : k + 1, :] = most(
            real & ((asked >> 3) == place) & ((asked & 1) == k),
            ((asked >> 1) & 3) * 16 + (rows_at >> 2),
            0,
        )
    for k in range(2, 8):
        ask_v[k : k + 1, :] = jnp.zeros((1, 128), jnp.int32)
    mine = rows[group, pl.ds(pl.multiple_of(lane * NZ, NZ), NZ), :]
    ask_v[8:16, :] = jnp.where((mine >> 6) == layer, ((mine >> 3) & 7) * 2 + (mine & 1), -1)
    spots = jnp.where(real & ((asked >> 6) == layer), ((asked >> 3) & 7) * 2 + (asked & 1), -1)
    for k in range(16):
        ask_v[16 + k : 17 + k, :] = most(spots == k, rows_at >> 2, 0)
    to_scalars(ask_v, ask, 0)

    def select(tile, l, k):
        return ask[k, l * NZ + tile]

    def unit_tables():
        wait_all(code_copies(2))
        unit_at, col = rows_at[:8], cols_at[:8]
        to = (col >> 1) * NL + ((row + group + layer) & 3) * 2 + (col & 1)
        come = jnp.full((1, 128), -1, jnp.int32)
        chosen = jnp.zeros((1, 128), jnp.int32)
        for g in range(ND):
            lay_rows(g)
            places = rows[g].T[64:72, :]
            head = ((col >> 3) & 1) * 8 + unit_at
            come = jnp.maximum(
                come, most((col < 64) & ((places >> 2) == place), (places & 3) * 16 + head, -1)
            )
            column = jnp.sum(
                jnp.where(col == lane * NZ + layer, places, 0), axis=1, keepdims=True
            )
            chosen = jnp.maximum(chosen, most((column >> 2) == to, g * 8 + unit_at, 0))
        from_z, from_l = rows_at & 7, rows_at >> 3
        via = (row - (from_l >> 1) - from_z + 16) & 3
        landing = (via * NL + from_l) * 2 + (from_z >> 2)
        came = jnp.broadcast_to(come, (128, 128)).T
        put_v[...] = jnp.zeros_like(put_v)
        put_v[0:1, :] = chosen
        put_v[1:2, :] = most(came == cols_at, landing, -1)
        to_scalars(put_v, put, 1)

    def kv_copy(i, r):
        return remote(
            kv_out.at[i, r],
            kv_in.at[i, lane],
            kv_send.at[i, r],
            kv_recv.at[i, r],
            at(group, layer, wrap(lane + r, NL)),
        )

    def kv_issue(i):
        tile = wrap(layer + OFFSETS[i], NZ)
        for k in range(2):
            code = select(tile, lane, k)
            kv_in[i, lane, 0, k] = mk_ref[code]
            kv_in[i, lane, 1, k] = mv_ref[code]

        @pl.loop(1, 8)
        def _(r):
            for k in range(2):
                code = select(tile, wrap(lane + r, NL), k)
                kv_out[i, r, 0, k] = mk_ref[code]
                kv_out[i, r, 1, k] = mv_ref[code]
            kv_copy(i, r).start()

    for load in loads:
        load.wait()
    for i in range(FIRST):
        kv_issue(i)

    def wz_copy(r, k):
        return remote(
            w_out.at[r, k],
            w_mid.at[k, lax.rem(layer, 4), lax.div(layer, 4)],
            wz_send.at[r, k],
            wz_recv.at[r, k],
            at(group, wrap(layer + r, NZ), lane),
        )

    def send_units():
        @pl.loop(1, 4)
        def _(r):
            x_copy(r).wait_recv()

        for r in range(8):
            to_layer = wrap(layer + r, NZ)
            for k in range(2):
                unit = put[0, to_layer * 2 + k]
                for kv in range(2):
                    slab = unit_all[unit // 8, unit % 8, kv]
                    if r == 0:
                        w_mid[k, lax.rem(layer, 4), lax.div(layer, 4), kv] = slab
                    else:
                        w_out[r, k, kv] = slab
                if r > 0:
                    wz_copy(r, k).start()

    def attend(qh, kh, vt, allowed=None):
        scores = (
            lax.dot_general(kh, qh, (((1,), (1,)), ((), ())), preferred_element_type=F32) * scale
        )
        if allowed is not None:
            scores = jnp.where(allowed, scores, NONE)
        top = jnp.max(scores, axis=0, keepdims=True)
        shifted = jnp.exp(scores - top)
        total = jnp.sum(shifted, axis=0, keepdims=True)
        out = jnp.dot(vt, shifted.astype(BF16), preferred_element_type=F32) * (1.0 / total)
        return out, top + jnp.log(total)

    def near(first):
        for h in range(first, first + 8):
            cols = slice(h * 128, h * 128 + 128)
            near_o[h], _ = attend(
                q_ref[:, cols], kl_ref[:, cols], vl_ref[:, cols].T, rows_at <= cols_at
            )
            cot_t[h] = cot_ref[:, cols].T

    for hop in range(4):
        q_copy(hop, True).wait_recv()
        if hop < 3:
            q_copy(hop + 1, True).start()
        q_copy(hop, False).wait_recv()
        if hop < 3:
            q_copy(hop + 1, False).start()
        if hop == UNITS_AFTER:
            unit_tables()
            send_units()
        if hop in (0, 1):
            near(8 * hop)

    def wy_copy(r):
        peer = wrap(lane + r, NL)
        low = wrap(lax.div(peer, 2) - row - group, 4)
        return remote(
            w_mid.at[lax.rem(peer, 2), low],
            w_in.at[group, lane],
            wy_send.at[r],
            wy_recv.at[r],
            at(group, layer, peer),
        )

    def wx_copy(r):
        return remote(
            w_in.at[group],
            w_in.at[group],
            wx_send.at[r],
            wx_recv.at[r],
            at(wrap(group + r, ND), layer, lane),
        )

    def result_copies(i, c):
        up = OFFSETS[i] > 0 or (OFFSETS[i] == -4 and c >= CHUNKS // 2)
        to = at(group, wrap(layer + (1 if up else -1), NZ), lane)
        return (
            remote(res_o.at[i, c], got_o.at[i, c], ro_send.at[i, c], ro_recv.at[i, c], to),
            remote(res_s.at[i, c], got_s.at[i, c], rs_send.at[i, c], rs_recv.at[i, c], to),
        )

    def pass_units():
        @pl.loop(1, 8)
        def _(r):
            for k in range(2):
                wz_copy(r, k).wait_recv()

        low = wrap(-group, 4)
        w_in[group, lane] = w_mid[lax.rem(lane, 2), low]

        @pl.loop(1, 8)
        def _(r):
            wy_copy(r).start()

        for k in range(FIRST, 8):
            kv_issue(k)

    if WY_AFTER < 0:
        pass_units()
    def joins(i, c):
        off = OFFSETS[i]
        if off == 0:
            return OFFSETS.index(1), OFFSETS.index(-1)
        if abs(off) == 3:
            return (0,) if (off > 0) == (c >= CHUNKS // 2) else ()
        return () if off == -4 else (OFFSETS.index(off + (1 if off > 0 else -1)),)

    for i, off in enumerate(OFFSETS):
        tile = wrap(layer + off, NZ)

        @pl.loop(1, 8)
        def _(r):
            kv_copy(i, r).wait_recv()

        @pl.loop(0, 4)
        def _(step):
            for k in range(4):
                s = step * 4 + k
                head = ask[16 + s, lane * NZ + tile]
                kh, vh = kv_in[i, step * 2 + k // 2, 0, k % 2], kv_in[i, step * 2 + k // 2, 1, k % 2]
                out, stat = attend(q_all[tile, head], kh, vh.T)
                slot_o[s] = out
                slot_s[s] = stat

        for c in range(CHUNKS):
            for j in joins(i, c):
                for copy in result_copies(j, c):
                    copy.wait_recv()

            @pl.loop(0, PART)
            def _(n):
                h = c * PART + n
                outs, stats = [], []
                for j in range(4):
                    where = ask[8 + tile, h * 4 + j]
                    spot = jnp.maximum(where, 0)
                    outs.append(slot_o[spot])
                    stats.append(jnp.where(where >= 0, slot_s[spot], NONE))
                for j in joins(i, c):
                    outs.append(got_o[j, c, n].astype(F32))
                    stats.append(got_s[j, c, pl.ds(n, 1), :])
                top = functools.reduce(jnp.maximum, stats)
                weights = [jnp.exp(stat - top) for stat in stats]
                total = functools.reduce(jnp.add, weights)
                inverse = 1.0 / total
                out = functools.reduce(
                    jnp.add, [(w * inverse) * o for w, o in zip(weights, outs)]
                )
                if off != 0:
                    res_o[i, c, n] = out.astype(BF16)
                    res_s[i, c, pl.ds(n, 1), :] = top + jnp.log(total)
                else:
                    cols = pl.ds(pl.multiple_of(h * 128, 128), 128)
                    opening = gate[h]
                    local = near_o[h]
                    mixed_ref[:, cols] = (opening * out + (1.0 - opening) * local).T.astype(BF16)
                    part[pl.ds(h, 1), :] = jnp.sum(
                        cot_t[h].astype(F32) * (out - local), axis=0, keepdims=True
                    )

            if off != 0:
                for copy in result_copies(i, c):
                    copy.start()

        if i == WY_AFTER:
            pass_units()

        if i == WX_AFTER:
            @pl.loop(1, 8)
            def _(r):
                wy_copy(r).wait_recv()

            @pl.loop(1, 4)
            def _(r):
                wx_copy(r).start()


    def spread(value, held, mine, size, s, r, to):
        held[mine] = value
        copies = [
            remote(held.at[mine], held.at[mine], s.at[k], r.at[k], to(k)) for k in range(1, size)
        ]
        for copy in copies:
            copy.start()
        return copies

    def total_of(held, copies):
        for copy in copies:
            copy.wait()
        return jnp.sum(held[...], axis=0)

    gx = spread(part[...], g_x, group, ND, gx_send, gx_recv, in_groups)

    @pl.loop(1, 4)
    def _(r):
        wx_copy(r).wait_recv()

    gl = spread(total_of(g_x, gx), g_l, lane, NL, gl_send, gl_recv, in_layer)

    @pl.loop(0, 64)
    def _(slab):
        where = put[1, slab]
        spot = jnp.maximum(where, 0)
        for kv, (old, new) in enumerate(((mk_ref, nk_ref), (mv_ref, nv_ref))):
            came = w_in[spot // 16, spot // 2 % 8, spot % 2, kv]
            new[slab] = jnp.where(where >= 0, came, old[slab])

    gz = spread(total_of(g_l, gl), g_z, layer, NZ, gz_send, gz_recv, along_z)

    for hop in range(4):
        q_copy(hop, True).wait_send()
        q_copy(hop, False).wait_send()
    for i, off in enumerate(OFFSETS):
        if off != 0:
            for c in range(CHUNKS):
                for copy in result_copies(i, c):
                    copy.wait_send()

        @pl.loop(1, 8)
        def _(r):
            kv_copy(i, r).wait_send()

    @pl.loop(1, 4)
    def _(r):
        x_copy(r).wait_send()
        wx_copy(r).wait_send()

    @pl.loop(1, 8)
    def _(r):
        wy_copy(r).wait_send()
        for k in range(2):
            wz_copy(r, k).wait_send()

    part_ref[...] = total_of(g_z, gz)


def on_device(
    queries,
    keys_local,
    values_local,
    mem_keys,
    mem_values,
    prev_keys,
    prev_values,
    gate_logit,
    cotangent,
    block_home,
    query_blocks,
    write_slots,
):
    own = codes(block_home, query_blocks, write_slots)
    sigmoid_gate = jax.nn.sigmoid(gate_logit)
    smem, vmem, later = (
        pl.BlockSpec(memory_space=space) for space in (pltpu.SMEM, pltpu.VMEM, pl.ANY)
    )
    dma = pltpu.SemaphoreType.DMA
    mixed, new_keys, new_values, part = pl.pallas_call(
        kernel,
        out_shape=(
            jax.ShapeDtypeStruct((128, 2048), BF16),
            jax.ShapeDtypeStruct((64, 128, 128), BF16),
            jax.ShapeDtypeStruct((64, 128, 128), BF16),
            jax.ShapeDtypeStruct((16, 128), F32),
        ),
        in_specs=[smem] + [vmem] * 2 + [later] * 5 + [vmem] * 2,
        out_specs=(vmem,) * 4,
        scratch_shapes=[
            pltpu.VMEM((128, 2048), BF16),
            pltpu.VMEM((128, 2048), BF16),
            pltpu.VMEM((128, 2048), BF16),
            pltpu.VMEM((64, 128, 128), BF16),
            pltpu.VMEM((64, 128, 128), BF16),
            pltpu.VMEM((ND, NL, NZ, 1, 128), jnp.int32),
            pltpu.VMEM((ND, 128, 128), jnp.int32),
            pltpu.VMEM((32, 128), jnp.int32),
            pltpu.SMEM((32, 128), jnp.int32),
            pltpu.VMEM((8, 128), jnp.int32),
            pltpu.SMEM((8, 128), jnp.int32),
            pltpu.VMEM((ND, 8, 2, 128, 128), BF16),
            pltpu.VMEM((8, 8, 2, 2, 128, 128), BF16),
            pltpu.VMEM((8, 8, 2, 2, 128, 128), BF16),
            pltpu.VMEM((8, 16, 128, 128), BF16),
            pltpu.VMEM((16, 128, 128), BF16),
            pltpu.VMEM((16, 128, 128), F32),
            pltpu.VMEM((16, 1, 128), F32),
            pltpu.VMEM((16, 128, 128), F32),
            pltpu.VMEM((7, CHUNKS, PART, 128, 128), BF16),
            pltpu.VMEM((7, CHUNKS, PART, 128), F32),
            pltpu.VMEM((7, CHUNKS, PART, 128, 128), BF16),
            pltpu.VMEM((7, CHUNKS, PART, 128), F32),
            pltpu.VMEM((8, 2, 2, 128, 128), BF16),
            pltpu.VMEM((2, 4, 2, 2, 128, 128), BF16),
            pltpu.VMEM((4, 8, 2, 2, 128, 128), BF16),
            pltpu.VMEM((16, 128), F32),
            pltpu.VMEM((ND, 16, 128), F32),
            pltpu.VMEM((NL, 16, 128), F32),
            pltpu.VMEM((NZ, 16, 128), F32),
            dma((5,)),
            dma((3, 8)),
            dma((3, 8)),
            dma((2,)),
            dma((ND,)),
            dma((ND,)),
            dma((8, 8)),
            dma((8, 8)),
            dma((2, 4)),
            dma((2, 4)),
            dma((7, CHUNKS)),
            dma((7, CHUNKS)),
            dma((7, CHUNKS)),
            dma((7, CHUNKS)),
            dma((8, 2)),
            dma((8, 2)),
            dma((8,)),
            dma((8,)),
            dma((4,)),
            dma((4,)),
            dma((ND,)),
            dma((ND,)),
            dma((NL,)),
            dma((NL,)),
            dma((NZ,)),
            dma((NZ,)),
        ],
        compiler_params=pltpu.CompilerParams(
            collective_id=0, has_side_effects=True, vmem_limit_bytes=60 * 1024 * 1024
        ),
    )(
        sigmoid_gate,
        own,
        queries,
        keys_local,
        values_local,
        cotangent,
        mem_keys.reshape(64, 128, 128),
        mem_values.reshape(64, 128, 128),
        prev_keys,
        prev_values,
    )
    total = jnp.sum(part, axis=1)
    gate_grad = sigmoid_gate * (1.0 - sigmoid_gate) * total
    return mixed, new_keys.reshape(mem_keys.shape), new_values.reshape(mem_values.shape), gate_grad


def solution(mesh):
    tokens, slabs = P(("dp", "mem"), None), P("mem", None, None, None)
    units = P(("dp", "mem"), None, None)
    return jax.shard_map(
        on_device,
        mesh=mesh,
        in_specs=(
            tokens,
            tokens,
            tokens,
            slabs,
            slabs,
            units,
            units,
            P(),
            tokens,
            P(),
            units,
            P(("dp", "mem")),
        ),
        out_specs=(tokens, slabs, slabs, P()),
        check_vma=False,
    )
```
